32 devices in a mesh: parts: 2 (over x), lon: 16 (over z, y, core).
Axes of the slice: x: 2, y: 2, z: 4, core: 2. Of those that a mesh axis runs over, the one named last changes fastest.
Arguments:
- carry_adjoint: float32 [32, 384, 2048], P('parts', 'lon'), parts along dimension 0, may hold values from -6 to 6
- east_courant: bfloat16 [32, 384, 2048], P('parts', 'lon'), parts along dimension 0, may hold values from -0.25 to 0.25
- north_courant: bfloat16 [32, 384, 2048], P('parts', 'lon'), parts along dimension 0, may hold values from -0.25 to 0.25
- sound_tile: int32 [32768, 1], P(('parts', 'lon')), parts along dimension 0, may hold values from 0 to 15; in each aligned block of 1024 rows (0 to 1023, 1024 to 2047, ...) at most 256 rows name the same one
- sound_cell: int32 [32768], P(('parts', 'lon')), parts along dimension 0, may hold values from 0 to 49151
- sound_kernel: float32 [32, 16384], P('parts', 'lon'), parts along dimension 0, may hold values from 0.2 to 1.5
- sound_weight: float32 [32768], P(('parts', 'lon')), parts along dimension 0, may hold values from -6 to 6
- cutoff: int32 [128], replicated, may hold values from 1 to 63, as said below
Outputs:
- initial_adjoint: float32 [32, 384, 2048], P('parts', 'lon'), parts along dimension 0
- flux_grad: float32 [768, 2048], P(('parts', 'lon')), parts along dimension 0
The draws below stay inside these ranges and needn't reach their ends.
There are 2 independent parts, one for each index of `parts`. The reference program is written for one: setup_inputs(seed, part) draws one part's arguments, and reference() takes and returns one part's arrays. A program takes and returns all parts, laid end to end along the dimension named above; an argument that names none is the same for every part. Nothing has to cross between parts.
Inputs may be any that keep to these rules, and one draw needn't show every extreme that they name: `sound_tile`: among the soundings of one orbit segment (aligned blocks of 1024), at most 256 lie in the same tile. `cutoff`: entries 0 to 63 belong to the southern cap from the pole, the rest to the northern cap toward the pole.
All inputs are finite; a program needn't handle non-finite values.
Results may differ from the reference program's by a relative error of at most 0.0009.
Values may be sent and summed in bfloat16 or wider, within the bound.
A program may use at most 128 MiB of HBM per device.

```python
import math
import jax
import jax.numpy as jnp
import numpy as np
from jax import lax

LEV = 16
LON_DEV = 24
NLAT = 2048
POLAR = 64
KMAX = 64
S_DEV = 1024
NLON = 384
SOUNDINGS = 16384
CAP = 256
N_LON = 16


def draw_cutoff(key, part):
    values = jax.random.randint(key, (2 * POLAR,), 1, KMAX)
    values = values.at[0].set(KMAX - 1)
    values = values.at[2 * POLAR - 1].set(1)
    return values.astype(jnp.int32)


def place_ends(array, own_key, smallest, top_value):
    dims = array.shape
    spot = [jax.random.randint(jax.random.fold_in(own_key, axis), (), 0, dims[axis]) for axis in range(len(dims))]
    array = array.at[tuple(spot)].set(smallest)
    longest = dims.index(max(dims))
    spot[longest] = (spot[longest] + 1) % dims[longest]
    return array.at[tuple(spot)].set(top_value)


def block_scale(rng, shape, split, least, high):
    level, own = 1.0, jax.random.fold_in(rng, 6)
    for axis_at, shards_of in split:
        draws = jnp.exp(jax.random.uniform(jax.random.fold_in(own, axis_at), (shards_of,), jnp.float32, least / len(split), high / len(split)))
        level = level * jnp.repeat(draws, shape[axis_at] // shards_of).reshape([-1 if axis == axis_at else 1 for axis in range(len(shape))])
    return level


def routed_block(rng, own, number, rows, amount, top, reach, slope):
    ranking = jax.random.permutation(rng, amount)
    packed, common = portions_of(amount, rows * top, reach, slope, True), portions_of(amount, rows * top, reach, slope, False)
    places = jnp.arange(amount)

    def named(sizes, rotation):
        used = int((sizes > 0).sum())
        fixed = max(1, used // 4)
        passed = fixed + (places - fixed + rotation * (used - fixed)) % max(1, amount - fixed)
        return jnp.zeros((amount,), jnp.int32).at[ranking[jnp.where(places < fixed, places, passed)]].set(jnp.asarray(sizes, jnp.int32))

    sizes = jnp.where(number % 4 == 0, named(packed, number // 4), named(common, number - number // 4 - 1))
    mixed = jax.random.permutation(jax.random.fold_in(own, 3), amount)
    donor, sink = mixed[0:amount // 2 * 2:2], mixed[1:amount // 2 * 2:2]
    margin = jnp.minimum(sizes[donor] - 1, reach - sizes[sink]) // 2
    margin = jnp.where((donor == ranking[0]) | (sink == ranking[0]) | (sizes[sink] == 0), 0, jnp.maximum(margin, 0))
    passed = jax.random.randint(jax.random.fold_in(own, 4), (amount // 2,), 0, 1 << 20) % (margin + 1)
    sizes = sizes.at[donor].add(-passed).at[sink].add(passed)
    labels = jnp.searchsorted(jnp.cumsum(sizes), jnp.arange(rows * top), side="right").astype(jnp.int32)
    table = labels.reshape(top, rows).T
    table = table[jax.random.permutation(jax.random.fold_in(own, 1), rows)]
    rotation = jax.random.randint(jax.random.fold_in(own, 2), (rows, 1), 0, top)
    return jnp.take_along_axis(table, (jnp.arange(top)[None, :] + rotation) % top, axis=1)


def portions_of(count, total, limit, skew, full):
    weights = [(1 << 20) // math.isqrt(rank ** skew) + 1 for rank in range(1, count + 1)]
    largest = limit if full else min(limit, max(-(-total // count), total * weights[0] // sum(weights)))
    least = 1 if total - largest >= count - 1 else 0
    counts, spare = [largest] + [least] * (count - 1), total - largest - least * (count - 1)
    while spare > 0:
        free = [i for i in range(1, count) if counts[i] < largest] or [i for i in range(1, count) if counts[i] < limit]
        pool, left = sum([weights[i] for i in free]), spare
        for i in free:
            more = min(limit - counts[i], max(1, left * weights[i] // pool), spare)
            counts[i] = counts[i] + more
            spare = spare - more
    return np.array(counts)


def bell_draw(stream_key, shape, spread, reach, shards=(), kind=jnp.bfloat16):
    factor_of = block_scale(stream_key, shape, shards, -0.22, 0.18) if shards else 1.0
    array = jax.random.normal(stream_key, shape, jnp.float32) * spread * factor_of
    return jnp.minimum(jnp.maximum(array, -reach), reach).astype(kind)


def setup_inputs(seed: int = 0, part: int = 0) -> dict:
    splits = jax.random.split(jax.random.key(seed), 9)
    part_splits = jax.random.split(jax.random.fold_in(splits[8], part), 9)
    carry_adjoint = bell_draw(part_splits[0], (LEV, NLON, NLAT), 1.0, 6.0, ((1, 16),), jnp.float32)
    east_courant = jnp.clip(jax.random.uniform(part_splits[1], (LEV, NLON, NLAT), jnp.float32, -0.25, 0.25) * block_scale(part_splits[1], (LEV, NLON, NLAT), ((1, 16),), -0.4, 0.0), -0.25, 0.25).astype(jnp.bfloat16)
    north_courant = jnp.clip(jax.random.uniform(part_splits[2], (LEV, NLON, NLAT), jnp.float32, -0.25, 0.25) * block_scale(part_splits[2], (LEV, NLON, NLAT), ((1, 16),), -0.4, 0.0), -0.25, 0.25).astype(jnp.bfloat16)
    sound_tile_keys = jax.random.split(jax.random.fold_in(part_splits[3], 1), SOUNDINGS // S_DEV)
    sound_tile_turns = jax.random.permutation(jax.random.fold_in(part_splits[3], 3), SOUNDINGS // S_DEV)
    sound_tile = jax.vmap(lambda own, number: routed_block(jax.random.fold_in(part_splits[3], 2), own, number, S_DEV, N_LON, 1, CAP, 2))(sound_tile_keys, sound_tile_turns).reshape((SOUNDINGS, 1))
    sound_cell = place_ends(jax.random.randint(part_splits[4], (SOUNDINGS,), 0, LON_DEV * NLAT), jax.random.fold_in(part_splits[4], 1), 0, (LON_DEV * NLAT) - 1).astype(jnp.int32)
    sound_kernel = jnp.clip(0.2 + 1.3 * jax.random.uniform(part_splits[5], (LEV, SOUNDINGS), jnp.float32) ** block_scale(part_splits[5], (LEV, SOUNDINGS), ((1, 16),), -0.2, 0.2), 0.2, 1.5)
    sound_weight = bell_draw(part_splits[6], (SOUNDINGS,), 1.0, 6.0, ((0, 16),), jnp.float32)
    cutoff = draw_cutoff(jax.random.fold_in(splits[8], 71), part)
    return dict(carry_adjoint=carry_adjoint, east_courant=east_courant, north_courant=north_courant, sound_tile=sound_tile, sound_cell=sound_cell, sound_kernel=sound_kernel, sound_weight=sound_weight, cutoff=cutoff)


def spectral_filter(field, cutoff):
    nlon = field.shape[0]
    polar = jnp.concatenate([field[:, :POLAR], field[:, NLAT - POLAR:]], axis=1)
    spectrum = jnp.fft.rfft(polar, axis=0)
    waves = jnp.arange(nlon // 2 + 1, dtype=jnp.int32)
    keep = waves[:, None] <= cutoff[None, :]
    smooth = jnp.fft.irfft(jnp.where(keep, spectrum, 0.0), n=nlon, axis=0).astype(field.dtype)
    return jnp.concatenate([smooth[:, :POLAR], field[:, POLAR:NLAT - POLAR], smooth[:, POLAR:]], axis=1)


def transport(field, east, west, north, south):
    right = jnp.roll(field, -1, axis=0)
    left = jnp.roll(field, 1, axis=0)
    column = jnp.zeros_like(field[:, :1])
    upper = jnp.concatenate([field[:, 1:], column], axis=1)
    lower = jnp.concatenate([column, field[:, :-1]], axis=1)
    out = field + jnp.maximum(east, 0.0) * (right - field) + jnp.minimum(west, 0.0) * (field - left)
    return out + jnp.maximum(north, 0.0) * (upper - field) + jnp.minimum(south, 0.0) * (field - lower)


def reference(carry_adjoint, east_courant, north_courant, sound_tile, sound_cell, sound_kernel, sound_weight, cutoff):
    nlon = carry_adjoint.shape[1]
    longitude = sound_tile[:, 0] * LON_DEV + sound_cell // NLAT
    flat_index = (longitude * NLAT + sound_cell % NLAT).astype(jnp.int32)
    values = sound_kernel * sound_weight[None, :]
    forcing = jnp.zeros((LEV, nlon * NLAT), carry_adjoint.dtype).at[:, flat_index].add(values)
    final_adjoint = carry_adjoint + forcing.reshape(LEV, nlon, NLAT)
    rows_index = jnp.arange(NLAT, dtype=jnp.int32)

    def one_level(items):
        field, east_bf, north_bf = items
        east = east_bf.astype(field.dtype)
        west = jnp.roll(east, 1, axis=0)
        north = jnp.where(rows_index[None, :] < NLAT - 1, north_bf.astype(field.dtype), 0.0)
        south = jnp.concatenate([jnp.zeros_like(north[:, :1]), north[:, :-1]], axis=1)
        middle = transport(spectral_filter(field, cutoff), east, west, north, south)
        start = transport(spectral_filter(middle, cutoff), east, west, north, south)
        return start, middle

    initial_adjoint, mid_adjoint = lax.map(one_level, (final_adjoint, east_courant, north_courant))
    flux_grad = final_adjoint[0] + mid_adjoint[0]
    return initial_adjoint, flux_grad
```

```python
import functools
import math

import jax
import jax.numpy as jnp
import numpy as np
from jax import lax
from jax.experimental import pallas as pl
from jax.experimental.pallas import tpu as pltpu
from jax.sharding import PartitionSpec as P

POLAR = 64
KMAX = 64
CAPS = 256
KEEP = 66
FIELDS = 32

HIGH = lax.Precision.HIGHEST
VMEM = pltpu.VMEM
BF = jnp.bfloat16
F32 = jnp.float32


def nt_dot(a, b):
    return lax.dot_general(a, b, (((1,), (1,)), ((), ())), preferred_element_type=F32)


def route_kernel(lanes, slots, tile_ref, cell_ref, kernel_ref, weight_ref, east_ref, north_ref,
                 message_ref, caps_ref, right_ref, left_ref):
    levels, width, rows = east_ref.shape
    count = tile_ref.shape[1]
    tile = tile_ref[...]
    cell = cell_ref[...]
    member = lax.broadcasted_iota(jnp.int32, (lanes, count), 0) == tile
    onehot = jnp.where(member, 1.0, 0.0)
    before = lax.broadcasted_iota(jnp.int32, (count, count), 0) < lax.broadcasted_iota(
        jnp.int32, (count, count), 1
    )
    earlier = jnp.dot(
        onehot.astype(BF), jnp.where(before, 1.0, 0.0).astype(BF), preferred_element_type=F32
    )
    rank = jnp.sum(onehot * earlier, axis=0, keepdims=True).astype(jnp.int32)
    place = lax.broadcasted_iota(jnp.int32, (slots, count), 0) == rank
    place = jnp.where(place, 1.0, 0.0).astype(BF)
    values = kernel_ref[...] * weight_ref[...]
    lon = cell // rows
    row = cell - lon * rows
    high = row // 128
    low = row - high * 128
    index = lax.broadcasted_iota(jnp.int32, (FIELDS - levels, count), 0)
    extra = jnp.where(index == 0, lon, jnp.where(index == 1, high, jnp.where(index == 2, low, 0)))
    fields = jnp.concatenate([values, extra.astype(F32)], axis=0)
    spread = [jnp.where(tile == d, fields, 0.0).astype(BF) for d in range(lanes)]
    routed = nt_dot(jnp.concatenate(spread, axis=0), place)
    message_ref[...] = routed.astype(BF).reshape(lanes, FIELDS, slots)
    half = CAPS // 2
    caps_ref[:, 0, :, :half] = east_ref[:, :, :half]
    caps_ref[:, 0, :, half:] = east_ref[:, :, rows - half :]
    caps_ref[:, 1, :, :half] = north_ref[:, :, :half]
    caps_ref[:, 1, :, half:] = north_ref[:, :, rows - half :]
    right_ref[0] = east_ref[:, width - 2, :]
    right_ref[1] = east_ref[:, width - 1, :]
    right_ref[2] = north_ref[:, width - 1, :]
    left_ref[0] = east_ref[:, 0, :]
    left_ref[1] = north_ref[:, 0, :]


def scatter_kernel(arrived_ref, carry_ref, final_ref, right_ref, left_ref, spread_ref, row_ref):
    levels, width, block = carry_ref.shape
    sources, _, slots = arrived_ref.shape

    @pl.when(pl.program_id(0) == 0)
    def _():
        for d in range(sources):
            part = arrived_ref[d].astype(F32)
            at = pl.ds(d * slots, slots)
            lon = part[levels : levels + 1]
            row_ref[:, at] = part[levels + 1 : levels + 2] * 128.0 + part[levels + 2 : levels + 3]
            here = lax.broadcasted_iota(jnp.int32, (width, slots), 0).astype(F32) == lon
            for l in range(levels):
                spread_ref[l * width : (l + 1) * width, at] = jnp.where(
                    here, part[l : l + 1], 0.0
                ).astype(BF)

    base = pl.program_id(0) * block
    row_index = (lax.broadcasted_iota(jnp.int32, (block, sources * slots), 0) + base).astype(F32)
    onehot = jnp.where(row_index == row_ref[...], 1.0, 0.0).astype(BF)
    forcing = nt_dot(spread_ref[...], onehot)
    final = carry_ref[...] + forcing.reshape(levels, width, block)
    final_ref[...] = final
    right_ref[0] = final[:, width - 2, :]
    right_ref[1] = final[:, width - 1, :]
    left_ref[0] = final[:, 0, :]
    left_ref[1] = final[:, 1, :]


def along_rows(field, north):
    rows = field.shape[-1]
    axis = field.ndim - 1
    step = pltpu.roll(field, rows - 1, axis) - field
    lower = pltpu.roll(jnp.minimum(north, 0.0) * step, 1, axis)
    return jnp.maximum(north, 0.0) * step + lower


def closed(north):
    rows = north.shape[-1]
    row = lax.broadcasted_iota(jnp.int32, north.shape, north.ndim - 1)
    return jnp.where(row < rows - 1, north.astype(F32), 0.0)


def polar_kernel(field_ref, courant_ref, cut_ref, table_ref, wide_ref, back_ref):
    sources, width, lanes = field_ref.shape
    nlon = sources * width
    field = field_ref[...].astype(F32).reshape(nlon, lanes)
    east = courant_ref[:, 0].astype(F32).reshape(nlon, lanes)
    north = closed(courant_ref[:, 1].astype(F32).reshape(nlon, lanes))
    wave = lax.broadcasted_iota(jnp.int32, (2 * KMAX, lanes), 0)
    wave = jnp.where(wave >= KMAX, wave - KMAX, wave)
    factor = jnp.where(wave == 0, 1.0 / nlon, 2.0 / nlon)
    scale = jnp.where(wave <= cut_ref[...], factor, 0.0)
    lane = lax.broadcasted_iota(jnp.int32, (nlon, lanes), 1)
    polar = (lane < POLAR) | (lane >= lanes - POLAR)

    def step(value):
        coef = jnp.dot(wide_ref[...], value, precision=HIGH, preferred_element_type=F32)
        smooth = jnp.dot(table_ref[...], coef * scale, precision=HIGH, preferred_element_type=F32)
        value = jnp.where(polar, smooth, value)
        change = pltpu.roll(value, nlon - 1, 0) - value
        west = pltpu.roll(jnp.minimum(east, 0.0) * change, 1, 0)
        return value + jnp.maximum(east, 0.0) * change + west + along_rows(value, north)

    middle = step(field)
    back_ref[:, 0] = step(middle).reshape(sources, width, lanes)
    back_ref[:, 1] = (field + middle).reshape(sources, width, lanes)


def band_kernel(final_ref, east_ref, north_ref, west_ref, right_ref, west_courant_ref,
                right_courant_ref, own_ref, own_courant_ref, initial_ref, flux_ref, edge_ref):
    levels, width, rows = final_ref.shape

    def up(x):
        return jnp.maximum(x, 0.0)

    def down(x):
        return jnp.minimum(x, 0.0)

    @pl.when(pl.program_id(0) == 0)
    def _():
        near, far = west_ref[1], west_ref[0]
        own_first, own_last = own_ref[0], own_ref[1]
        change = own_first - near
        e_near = west_courant_ref[1].astype(F32)
        from_near = down(e_near) * change
        before = near + up(e_near) * change + down(west_courant_ref[0].astype(F32)) * (near - far)
        edge_ref[0] = from_near
        edge_ref[1] = before + along_rows(near, closed(west_courant_ref[2]))
        after, beyond = right_ref[0], right_ref[1]
        e_after = right_courant_ref[0].astype(F32)
        next_mid = after + up(e_after) * (beyond - after)
        next_mid += down(own_courant_ref[...].astype(F32)) * (after - own_last)
        edge_ref[2] = next_mid + along_rows(after, closed(right_courant_ref[1]))
        edge_ref[3] = after
        edge_ref[4] = down(e_near)

    def level(l, _):
        field = final_ref[l]
        east = east_ref[l].astype(F32)
        north = closed(north_ref[l])
        at = lax.broadcasted_iota(jnp.int32, (width, rows), 0)
        row = pl.ds(pl.program_id(0) * levels + l, 1)

        def step(value, right, west):
            right = jnp.where(at == width - 1, right, pltpu.roll(value, width - 1, 0))
            change = right - value
            west = jnp.where(at == 0, west, pltpu.roll(down(east) * change, 1, 0))
            return value + up(east) * change + west + along_rows(value, north)

        middle = step(field, edge_ref[3, row], edge_ref[0, row])
        west = edge_ref[4, row] * (middle[0:1] - edge_ref[1, row])
        initial_ref[l] = step(middle, edge_ref[2, row], west)

        @pl.when((pl.program_id(0) == 0) & (l == 0))
        def _():
            flux_ref[...] = field + middle

        return 0

    lax.fori_loop(0, levels, level, 0)


def merge_kernel(initial_ref, flux_ref, back_ref, flux_back_ref, initial_out, flux_out):
    second = pl.program_id(0)
    half = initial_ref.shape[-1]

    def inside(shape):
        lane = lax.broadcasted_iota(jnp.int32, shape, len(shape) - 1)
        return jnp.where(second == 1, half - 1 - lane, lane) < KEEP

    initial_out[...] = jnp.where(
        inside(initial_ref.shape), back_ref[:, 0].astype(F32), initial_ref[...]
    )
    flux_out[...] = jnp.where(inside(flux_ref.shape), flux_back_ref[...].astype(F32), flux_ref[...])


def full_table(nlon):
    phase = np.arange(nlon)[:, None] * np.arange(KMAX)[None, :] % nlon
    angle = phase * (2.0 * math.pi / nlon)
    return np.concatenate([np.cos(angle), np.sin(angle)], axis=1).astype(np.float32)


LIMIT = 48 * 1024 * 1024


def params(**more):
    return pltpu.CompilerParams(vmem_limit_bytes=LIMIT, **more)


def cost(flops, moved):
    return pl.CostEstimate(flops=flops, bytes_accessed=moved, transcendentals=0)


def levels_spread(carry, east, north, sound_tile, sound_cell, sound_kernel, sound_weight, cutoff):
    levels, width, rows = carry.shape
    lanes = lax.axis_size("lon")
    count = sound_weight.shape[0]
    slots = max(2, 4 * count // lanes)
    half = CAPS // 2
    whole = pl.BlockSpec(memory_space=VMEM)
    shape = jax.ShapeDtypeStruct
    message, caps, to_right, to_left = pl.pallas_call(
        functools.partial(route_kernel, lanes, slots),
        out_shape=(
            shape((lanes, FIELDS, slots), BF),
            shape((levels, 2, width, CAPS), BF),
            shape((3, levels, rows), BF),
            shape((2, levels, rows), BF),
        ),
        in_specs=[whole] * 6,
        out_specs=(whole,) * 4,
        compiler_params=params(),
        name="route",
    )(
        sound_tile.reshape(1, count),
        sound_cell.reshape(1, count),
        sound_kernel,
        sound_weight.reshape(1, count),
        east,
        north,
    )
    arrived = lax.all_to_all(message, "lon", split_axis=0, concat_axis=0, tiled=True)
    up = [(i, (i + 1) % lanes) for i in range(lanes)]
    down = [(j, i) for i, j in up]
    west_courant = lax.ppermute(to_right, "lon", up)
    right_courant = lax.ppermute(to_left, "lon", down)
    courant = lax.all_to_all(caps, "lon", split_axis=0, concat_axis=0, tiled=True)
    block = 256
    final, right_edge, left_edge = pl.pallas_call(
        scatter_kernel,
        grid=(rows // block,),
        out_shape=(
            shape((levels, width, rows), F32),
            shape((2, levels, rows), F32),
            shape((2, levels, rows), F32),
        ),
        in_specs=[
            pl.BlockSpec((lanes, FIELDS, slots), lambda i: (0, 0, 0)),
            pl.BlockSpec((levels, width, block), lambda i: (0, 0, i)),
        ],
        out_specs=(
            pl.BlockSpec((levels, width, block), lambda i: (0, 0, i)),
            pl.BlockSpec((2, levels, block), lambda i: (0, 0, i)),
            pl.BlockSpec((2, levels, block), lambda i: (0, 0, i)),
        ),
        scratch_shapes=[
            VMEM((levels * width, lanes * slots), BF),
            VMEM((1, lanes * slots), F32),
        ],
        compiler_params=params(),
        name="scatter",
    )(arrived, carry)
    polar = jnp.concatenate([final[:, :, :half], final[:, :, rows - half :]], axis=2)
    gathered = lax.all_to_all(polar, "lon", split_axis=0, concat_axis=0, tiled=True)
    west = lax.ppermute(right_edge, "lon", up)
    right = lax.ppermute(left_edge, "lon", down)
    own = jnp.stack([left_edge[0], right_edge[1]])
    table = full_table(lanes * width)
    spare = jnp.zeros((CAPS - 2 * POLAR,), jnp.int32)
    cut = jnp.concatenate([cutoff[:POLAR], spare, cutoff[POLAR:]]).reshape(1, CAPS)
    back = pl.pallas_call(
        polar_kernel,
        out_shape=shape((lanes, 2, width, CAPS), F32),
        in_specs=[whole] * 5,
        out_specs=whole,
        compiler_params=params(),
        name="polar",
    )(gathered, courant, cut, jnp.asarray(table), jnp.asarray(table.T.copy()))
    returned = lax.all_to_all(back, "lon", split_axis=0, concat_axis=0, tiled=True)
    part = 4 if levels % 4 == 0 else levels
    tile = pl.BlockSpec((part, width, rows), lambda i: (i, 0, 0))

    def strip(n):
        return pl.BlockSpec((n, levels, rows), lambda i: (0, 0, 0))

    initial, flux = pl.pallas_call(
        band_kernel,
        grid=(levels // part,),
        out_shape=(shape((levels, width, rows), F32), shape((width, rows), F32)),
        in_specs=[tile, tile, tile, strip(2), strip(2), strip(3), strip(2), strip(2),
                  pl.BlockSpec((levels, rows), lambda i: (0, 0))],
        out_specs=(tile, pl.BlockSpec((width, rows), lambda i: (0, 0))),
        scratch_shapes=[VMEM((5, levels, rows), F32)],
        compiler_params=params(),
        cost_estimate=cost(40 * levels * width * rows, 12 * levels * width * rows),
        name="band",
    )(final, east, north, west, right, west_courant, right_courant, own, to_right[1])
    ends = rows // half - 1
    return pl.pallas_call(
        merge_kernel,
        grid=(2,),
        out_shape=(shape((levels, width, rows), F32), shape((width, rows), F32)),
        in_specs=[
            pl.BlockSpec((levels, width, half), lambda i: (0, 0, i * ends)),
            pl.BlockSpec((width, half), lambda i: (0, i * ends)),
            pl.BlockSpec((levels, 1, width, half), lambda i: (0, 0, 0, i)),
            pl.BlockSpec((None, None, width, half), lambda i: (0, 1, 0, i)),
        ],
        out_specs=(
            pl.BlockSpec((levels, width, half), lambda i: (0, 0, i * ends)),
            pl.BlockSpec((width, half), lambda i: (0, i * ends)),
        ),
        input_output_aliases={0: 0, 1: 1},
        compiler_params=params(),
        name="merge",
    )(initial, flux, returned, returned)


def extended(x, sides, width):
    for axis, dim in sides:
        devices, length = (lax.axis_size(axis), x.shape[dim])
        up = [(i, (i + 1) % devices) for i in range(devices)]
        down = [(j, i) for i, j in up]
        last = lax.slice_in_dim(x, length - width, length, axis=dim)
        initial = lax.slice_in_dim(x, 0, width, axis=dim)
        before = lax.ppermute(last, axis, up)
        after = lax.ppermute(initial, axis, down)
        x = jnp.concatenate([before, x, after], axis=dim)
    return x


def shifted(block, axis, distance):
    devices = range(lax.axis_size(axis))
    route = [((i - distance) % len(devices), i) for i in devices]
    return lax.ppermute(block, axis, route)


def wave_table(longitudes, nlon):
    waves = jnp.arange(KMAX, dtype=jnp.int32)
    phase = longitudes[:, None] * waves[None, :] % nlon
    angle = phase.astype(jnp.float32) * (2.0 * math.pi / nlon)
    return jnp.concatenate([jnp.cos(angle), jnp.sin(angle)], axis=1)


def wave_scale(cut_rows, nlon):
    waves = jnp.arange(KMAX, dtype=jnp.int32)
    factor = jnp.where(waves == 0, 1.0, 2.0) / nlon
    kept = jnp.where(waves[None, :] <= cut_rows[:, None], factor[None, :], 0.0).astype(jnp.float32)
    return jnp.concatenate([kept, kept], axis=1)


def spectral(polar, cutoff):
    levels, width, caps = polar.shape
    lanes = lax.axis_size("lon")
    me = lax.axis_index("lon")
    nlon = width * lanes
    table = wave_table(me * width + jnp.arange(width, dtype=jnp.int32), nlon)
    partial_coef = jnp.einsum("lwr,wk->lrk", polar, table, precision=HIGH)
    total = lax.psum(partial_coef, "lon")
    scale = wave_scale(cutoff, nlon)
    return jnp.einsum("lrk,wk->lwr", total * scale[None], table, precision=HIGH)


def transport(padded, east, west, north, south):
    field = padded[:, 1:-1]
    right = padded[:, 2:]
    left = padded[:, :-2]
    column = jnp.zeros_like(field[:, :, :1])
    upper = jnp.concatenate([field[:, :, 1:], column], axis=2)
    lower = jnp.concatenate([column, field[:, :, :-1]], axis=2)
    out = field + jnp.maximum(east, 0) * (right - field) + jnp.minimum(west, 0) * (field - left)
    return out + jnp.maximum(north, 0) * (upper - field) + jnp.minimum(south, 0) * (field - lower)


def adjoint_step(field, cutoff, east, west, north, south):
    rows = field.shape[2]
    polar = jnp.concatenate([field[:, :, :POLAR], field[:, :, rows - POLAR :]], axis=2)
    smooth = spectral(polar, cutoff)
    filtered = jnp.concatenate(
        [smooth[:, :, :POLAR], field[:, :, POLAR : rows - POLAR], smooth[:, :, POLAR:]], axis=2
    )
    padded = extended(filtered, (("lon", 1),), 1)
    return transport(padded, east, west, north, south)


def any_lanes(
    carry_adjoint,
    east_courant,
    north_courant,
    sound_tile,
    sound_cell,
    sound_kernel,
    sound_weight,
    cutoff,
):
    levels, width, rows = carry_adjoint.shape
    lanes = lax.axis_size("lon")
    count = sound_weight.shape[0]
    slots = max(2, 4 * count // lanes)
    target = sound_tile[:, 0]
    onehot = (target[:, None] == jnp.arange(lanes, dtype=jnp.int32)[None, :]).astype(jnp.int32)
    rank = jnp.sum((jnp.cumsum(onehot, axis=0) - 1) * onehot, axis=1)
    position = target * slots + rank
    values = sound_kernel * sound_weight[None, :]
    outgoing = jnp.zeros((levels, lanes * slots), jnp.float32).at[:, position].set(values)
    places = jnp.zeros((lanes * slots,), jnp.int32).at[position].set(sound_cell)
    arrived, spots = (
        lax.all_to_all(
            outgoing.reshape(levels, lanes, slots).astype(jnp.bfloat16),
            "lon",
            split_axis=1,
            concat_axis=1,
            tiled=True,
        ).astype(jnp.float32),
        lax.all_to_all(
            places.reshape(1, lanes, slots), "lon", split_axis=1, concat_axis=1, tiled=True
        ),
    )
    forcing = (
        jnp.zeros((levels, width * rows), jnp.float32)
        .at[:, spots.reshape(-1)]
        .add(arrived.reshape(levels, -1))
    )
    final_adjoint = carry_adjoint + forcing.reshape(levels, width, rows)
    west_face = shifted(east_courant[:, width - 1 :, :], "lon", 1)
    west_courant = jnp.concatenate([west_face, east_courant[:, :-1, :]], axis=1)
    row_index = jnp.arange(rows, dtype=jnp.int32)
    north = jnp.where(
        row_index[None, None, :] < rows - 1, north_courant, jnp.zeros_like(north_courant)
    )
    south = jnp.concatenate([jnp.zeros_like(north[:, :, :1]), north[:, :, :-1]], axis=2)
    mid_adjoint = adjoint_step(final_adjoint, cutoff, east_courant, west_courant, north, south)
    initial_adjoint = adjoint_step(mid_adjoint, cutoff, east_courant, west_courant, north, south)
    flux_grad = final_adjoint[0] + mid_adjoint[0]
    return (initial_adjoint, flux_grad)


def per_device(*arrays):
    if arrays[0].shape[0] == lax.axis_size("lon"):
        return levels_spread(*arrays)
    return any_lanes(*arrays)


def solution(mesh):
    in_specs = (
        P("parts", "lon", None),
        P("parts", "lon", None),
        P("parts", "lon", None),
        P(("parts", "lon"), None),
        P(("parts", "lon")),
        P("parts", "lon"),
        P(("parts", "lon")),
        P(),
    )
    out_specs = (P("parts", "lon", None), P(("parts", "lon"), None))
    return jax.shard_map(
        per_device, mesh=mesh, in_specs=in_specs, out_specs=out_specs, check_vma=False
    )
```

```python
import functools
import math

import jax
import jax.numpy as jnp
import numpy as np
from jax import lax
from jax.experimental import pallas as pl
from jax.experimental.pallas import tpu as pltpu
from jax.sharding import PartitionSpec as P

POLAR = 64
KMAX = 64
CAPS = 256
KEEP = 66
FIELDS = 32

HIGH = lax.Precision.HIGHEST
VMEM = pltpu.VMEM
BF = jnp.bfloat16
F32 = jnp.float32


def nt_dot(a, b):
    return lax.dot_general(a, b, (((1,), (1,)), ((), ())), preferred_element_type=F32)


def along_rows(field, north):
    rows = field.shape[-1]
    axis = field.ndim - 1
    step = pltpu.roll(field, rows - 1, axis) - field
    lower = pltpu.roll(jnp.minimum(north, 0.0) * step, 1, axis)
    return jnp.maximum(north, 0.0) * step + lower


def closed(north):
    rows = north.shape[-1]
    row = lax.broadcasted_iota(jnp.int32, north.shape, north.ndim - 1)
    return jnp.where(row < rows - 1, north.astype(F32), 0.0)


class Exchange:
    def __init__(self, lanes, send, receive, send_sem, receive_sem):
        self.lanes, self.send, self.receive = lanes, send, receive
        self.send_sem, self.receive_sem = send_sem, receive_sem
        self.me = lax.axis_index("lon")

    def copy(self, k, slot):
        target = lax.rem(self.me + k, self.lanes)
        return pltpu.make_async_remote_copy(
            src_ref=self.send.at[target],
            dst_ref=self.receive.at[slot],
            send_sem=self.send_sem.at[k],
            recv_sem=self.receive_sem.at[k],
            device_id={"lon": target},
            device_id_type=pl.DeviceIdType.MESH,
        )

    def start(self):
        def one(k, _):
            self.copy(k, self.me).start()
            return 0

        lax.fori_loop(1, self.lanes, one, 0)
        self.receive[self.me] = self.send[self.me]

    def arrive(self):
        def one(k, _):
            self.copy(k, lax.rem(self.me + self.lanes - k, self.lanes)).wait_recv()
            return 0

        lax.fori_loop(1, self.lanes, one, 0)

    def leave(self):
        def one(k, _):
            self.copy(k, self.me).wait_send()
            return 0

        lax.fori_loop(1, self.lanes, one, 0)


def window_kernel(tile_hbm, cell_hbm, kernel_hbm, weight_hbm, carry_hbm, east_hbm, north_hbm,
                  cut_hbm, table_hbm, wide_hbm, initial_hbm, flux_hbm,
                  tile_ref, cell_ref, kernel_ref, weight_ref, final_ref, east_ref, north_ref,
                  cut_ref, table_ref, wide_ref, message, arrived, caps, courant, ends, circles,
                  back, returned, flux_send, flux_caps, to_right, to_left, from_west, from_east,
                  right_edge, left_edge, west_edge, east_edge, spread_ref, row_ref, edge_ref,
                  initial_ref, flux_ref, load_sem, store_sem, all_send, all_receive, flux_sems,
                  side_send, side_receive):
    levels, width, rows = carry_hbm.shape
    lanes, _, slots = message.shape
    half = CAPS // 2
    block = 256
    me = lax.axis_index("lon")
    right, left = lax.rem(me + 1, lanes), lax.rem(me + lanes - 1, lanes)
    pairs = [(tile_hbm, tile_ref), (cell_hbm, cell_ref), (weight_hbm, weight_ref),
             (kernel_hbm, kernel_ref), (east_hbm, east_ref), (north_hbm, north_ref),
             (carry_hbm, final_ref), (cut_hbm, cut_ref), (table_hbm, table_ref),
             (wide_hbm, wide_ref)]
    loads = [pltpu.make_async_copy(a, b, load_sem.at[i]) for i, (a, b) in enumerate(pairs)]
    for load in loads:
        load.start()

    barrier = pltpu.get_barrier_semaphore()

    def greet(k, _):
        pl.semaphore_signal(
            barrier, inc=1, device_id={"lon": lax.rem(me + k, lanes)},
            device_id_type=pl.DeviceIdType.MESH,
        )
        return 0

    lax.fori_loop(1, lanes, greet, 0)

    def side(send, receive, sem, target):
        return pltpu.make_async_remote_copy(
            src_ref=send, dst_ref=receive, send_sem=side_send.at[sem],
            recv_sem=side_receive.at[sem], device_id={"lon": target},
            device_id_type=pl.DeviceIdType.MESH,
        )

    for load in loads[:4]:
        load.wait()
    route(tile_ref, cell_ref, kernel_ref, weight_ref, message, rows)
    pl.semaphore_wait(barrier, lanes - 1)
    soundings = Exchange(lanes, message, arrived, all_send.at[0], all_receive.at[0])
    soundings.start()

    for load in loads[4:6]:
        load.wait()
    caps[:, 0, :, :half] = east_ref[:, :, :half]
    caps[:, 0, :, half:] = east_ref[:, :, rows - half :]
    caps[:, 1, :, :half] = north_ref[:, :, :half]
    caps[:, 1, :, half:] = north_ref[:, :, rows - half :]
    winds = Exchange(lanes, caps, courant, all_send.at[1], all_receive.at[1])
    winds.start()
    to_right[0] = east_ref[:, width - 2, :]
    to_right[1] = east_ref[:, width - 1, :]
    to_right[2] = north_ref[:, width - 1, :]
    to_left[0] = east_ref[:, 0, :]
    to_left[1] = north_ref[:, 0, :]
    wind_sides = [side(to_right, from_west, 0, right), side(to_left, from_east, 1, left)]
    for copy in wind_sides:
        copy.start()

    soundings.arrive()
    for d in range(lanes):
        part = arrived[d]
        at = pl.ds(d * slots, slots)
        wide = part[levels : levels + 8].astype(F32)
        row_ref[:, at] = wide[1:2] * 128.0 + wide[2:3]
        here = lax.broadcasted_iota(jnp.int32, (width, slots), 0).astype(F32) == wide[0:1]
        values = part[:levels].astype(F32)
        for l in range(levels):
            spread_ref[l * width : (l + 1) * width, at] = jnp.where(
                here, values[l : l + 1], 0.0
            ).astype(BF)
    loads[6].wait()

    def scatter(base):
        at = pl.ds(base, block)
        row = row_ref[...] - jnp.asarray(base, F32)
        row = jnp.where((row >= 0) & (row < block), row, -1.0).astype(BF)
        index = lax.broadcasted_iota(jnp.int32, (block, lanes * slots), 0).astype(F32).astype(BF)
        onehot = jnp.where(index == row, jnp.ones((), BF), jnp.zeros((), BF))
        forcing = nt_dot(spread_ref[...], onehot)
        final_ref[:, :, at] = final_ref[:, :, at] + forcing.reshape(levels, width, block)

    scatter(0)
    scatter(rows - block)
    ends[:, :, :half] = final_ref[:, :, :half]
    ends[:, :, half:] = final_ref[:, :, rows - half :]
    polar = Exchange(lanes, ends, circles, all_send.at[2], all_receive.at[2])
    polar.start()

    def middle_block(i, _):
        scatter(pl.multiple_of(i * block, block))
        return 0

    lax.fori_loop(1, rows // block - 1, middle_block, 0)
    right_edge[0] = final_ref[:, width - 2, :]
    right_edge[1] = final_ref[:, width - 1, :]
    left_edge[0] = final_ref[:, 0, :]
    left_edge[1] = final_ref[:, 1, :]
    field_sides = [side(right_edge, west_edge, 2, right), side(left_edge, east_edge, 3, left)]
    for copy in field_sides:
        copy.start()

    for load in loads[7:]:
        load.wait()
    winds.arrive()
    polar.arrive()
    polar_steps(circles, courant, cut_ref, table_ref, wide_ref, back, flux_send)
    answer = Exchange(lanes, back, returned, all_send.at[3], all_receive.at[3])
    answer.start()

    def flux_copy(k):
        return pltpu.make_async_remote_copy(
            src_ref=flux_send.at[k], dst_ref=flux_caps, send_sem=flux_sems.at[k],
            recv_sem=flux_sems.at[0], device_id={"lon": k},
            device_id_type=pl.DeviceIdType.MESH,
        )

    @pl.when(me == 0)
    def _():
        def one(k, _):
            flux_copy(k).start()
            return 0

        lax.fori_loop(1, lanes, one, 0)
        flux_caps[...] = flux_send[0]

    for copy in wind_sides + field_sides:
        copy.wait_recv()
    side_edges(west_edge, east_edge, from_west, from_east, left_edge, right_edge, to_right, edge_ref)

    inner = pl.ds(half, rows - CAPS)

    def store(l):
        return pltpu.make_async_copy(
            initial_ref.at[l, :, inner], initial_hbm.at[l, :, inner], store_sem.at[l]
        )

    def level(l, _):
        middle = band(l, final_ref, east_ref, north_ref, edge_ref, initial_ref)
        store(l).start()

        @pl.when(l == 0)
        def _():
            flux_ref[...] = final_ref[0] + middle

        return 0

    lax.fori_loop(0, levels, level, 0)
    answer.arrive()

    @pl.when(me != 0)
    def _():
        flux_copy(1).wait_recv()

    lane = lax.broadcasted_iota(jnp.int32, (width, half), 1)
    lasts = []
    for i, at in enumerate((pl.ds(0, half), pl.ds(rows - half, half))):
        inside = (lane if i == 0 else half - 1 - lane) < KEEP
        side_at = pl.ds(i * half, half)
        for l in range(levels):
            initial_ref[l, :, at] = jnp.where(inside, returned[l, :, side_at], initial_ref[l, :, at])
        flux_ref[:, at] = jnp.where(inside, flux_caps[:, side_at], flux_ref[:, at])
        lasts.append(pltpu.make_async_copy(
            initial_ref.at[:, :, at], initial_hbm.at[:, :, at], store_sem.at[levels + i]
        ))
        lasts[-1].start()
    lasts.append(pltpu.make_async_copy(flux_ref, flux_hbm, store_sem.at[levels + 2]))
    lasts[-1].start()

    for copy in wind_sides + field_sides:
        copy.wait_send()
    for exchange in (soundings, winds, polar, answer):
        exchange.leave()

    @pl.when(me == 0)
    def _():
        def one(k, _):
            flux_copy(k).wait_send()
            return 0

        lax.fori_loop(1, lanes, one, 0)

    def stored(l, _):
        store(l).wait()
        return 0

    lax.fori_loop(0, levels, stored, 0)
    for copy in lasts:
        copy.wait()


def route(tile_ref, cell_ref, kernel_ref, weight_ref, message, rows):
    lanes, _, slots = message.shape
    levels, count = kernel_ref.shape
    tile = tile_ref[...]
    cell = cell_ref[...]
    member = lax.broadcasted_iota(jnp.int32, (lanes, count), 0) == tile
    onehot = jnp.where(member, 1.0, 0.0)
    before = lax.broadcasted_iota(jnp.int32, (count, count), 0) < lax.broadcasted_iota(
        jnp.int32, (count, count), 1
    )
    earlier = jnp.dot(
        onehot.astype(BF), jnp.where(before, 1.0, 0.0).astype(BF), preferred_element_type=F32
    )
    rank = jnp.sum(onehot * earlier, axis=0, keepdims=True).astype(jnp.int32)
    place = lax.broadcasted_iota(jnp.int32, (slots, count), 0) == rank
    place = jnp.where(place, 1.0, 0.0).astype(BF)
    values = kernel_ref[...] * weight_ref[...]
    lon = cell // rows
    row = cell - lon * rows
    high = row // 128
    low = row - high * 128
    index = lax.broadcasted_iota(jnp.int32, (FIELDS - levels, count), 0)
    extra = jnp.where(index == 0, lon, jnp.where(index == 1, high, jnp.where(index == 2, low, 0)))
    fields = jnp.concatenate([values, extra.astype(F32)], axis=0)
    spread = [jnp.where(tile == d, fields, 0.0).astype(BF) for d in range(lanes)]
    routed = nt_dot(jnp.concatenate(spread, axis=0), place)
    message[...] = routed.astype(BF).reshape(lanes, FIELDS, slots)


def polar_steps(field_ref, courant_ref, cut_ref, table_ref, wide_ref, back_ref, flux_send):
    sources, width, lanes = field_ref.shape
    nlon = sources * width
    field = field_ref[...].reshape(nlon, lanes)
    east = courant_ref[:, 0].astype(F32).reshape(nlon, lanes)
    north = closed(courant_ref[:, 1].astype(F32).reshape(nlon, lanes))
    wave = lax.broadcasted_iota(jnp.int32, (2 * KMAX, lanes), 0)
    wave = jnp.where(wave >= KMAX, wave - KMAX, wave)
    factor = jnp.where(wave == 0, 1.0 / nlon, 2.0 / nlon)
    scale = jnp.where(wave <= cut_ref[...], factor, 0.0)
    lane = lax.broadcasted_iota(jnp.int32, (nlon, lanes), 1)
    polar = (lane < POLAR) | (lane >= lanes - POLAR)

    def step(value):
        coef = jnp.dot(wide_ref[...], value, precision=HIGH, preferred_element_type=F32)
        smooth = jnp.dot(table_ref[...], coef * scale, precision=HIGH, preferred_element_type=F32)
        value = jnp.where(polar, smooth, value)
        change = pltpu.roll(value, nlon - 1, 0) - value
        west = pltpu.roll(jnp.minimum(east, 0.0) * change, 1, 0)
        return value + jnp.maximum(east, 0.0) * change + west + along_rows(value, north)

    middle = step(field)
    flux_send[...] = (field + middle).reshape(sources, width, lanes)
    back_ref[...] = step(middle).reshape(sources, width, lanes)


def up(x):
    return jnp.maximum(x, 0.0)


def down(x):
    return jnp.minimum(x, 0.0)


def side_edges(west_ref, right_ref, west_courant_ref, right_courant_ref, left_edge, right_edge,
               to_right, edge_ref):
    near, far = west_ref[1], west_ref[0]
    own_first, own_last = left_edge[0], right_edge[1]
    change = own_first - near
    e_near = west_courant_ref[1].astype(F32)
    from_near = down(e_near) * change
    before = near + up(e_near) * change + down(west_courant_ref[0].astype(F32)) * (near - far)
    edge_ref[0] = from_near
    edge_ref[1] = before + along_rows(near, closed(west_courant_ref[2]))
    after, beyond = right_ref[0], right_ref[1]
    e_after = right_courant_ref[0].astype(F32)
    next_mid = after + up(e_after) * (beyond - after)
    next_mid += down(to_right[1].astype(F32)) * (after - own_last)
    edge_ref[2] = next_mid + along_rows(after, closed(right_courant_ref[1]))
    edge_ref[3] = after
    edge_ref[4] = down(e_near)


def band(l, final_ref, east_ref, north_ref, edge_ref, initial_ref):
    levels, width, rows = final_ref.shape
    row = pl.ds(l, 1)
    field = final_ref[l]
    east = east_ref[l].astype(F32)
    north = closed(north_ref[l])
    at = lax.broadcasted_iota(jnp.int32, (width, rows), 0)

    def step(value, right, west):
        right = jnp.where(at == width - 1, right, pltpu.roll(value, width - 1, 0))
        change = right - value
        west = jnp.where(at == 0, west, pltpu.roll(down(east) * change, 1, 0))
        return value + up(east) * change + west + along_rows(value, north)

    middle = step(field, edge_ref[3, row], edge_ref[0, row])
    west = edge_ref[4, row] * (middle[0:1] - edge_ref[1, row])
    initial_ref[l] = step(middle, edge_ref[2, row], west)
    return middle


def full_table(nlon):
    phase = np.arange(nlon)[:, None] * np.arange(KMAX)[None, :] % nlon
    angle = phase * (2.0 * math.pi / nlon)
    return np.concatenate([np.cos(angle), np.sin(angle)], axis=1).astype(np.float32)


LIMIT = 56 * 1024 * 1024


def levels_spread(carry, east, north, sound_tile, sound_cell, sound_kernel, sound_weight, cutoff):
    levels, width, rows = carry.shape
    lanes = lax.axis_size("lon")
    nlon = lanes * width
    count = sound_weight.shape[0]
    slots = max(2, 4 * count // lanes)
    shape = jax.ShapeDtypeStruct
    table = full_table(nlon)
    spare = jnp.zeros((CAPS - 2 * POLAR,), jnp.int32)
    cut = jnp.concatenate([cutoff[:POLAR], spare, cutoff[POLAR:]]).reshape(1, CAPS)
    anywhere = pl.BlockSpec(memory_space=pl.ANY)
    return pl.pallas_call(
        window_kernel,
        out_shape=(shape((levels, width, rows), F32), shape((width, rows), F32)),
        in_specs=[anywhere] * 10,
        out_specs=(anywhere,) * 2,
        scratch_shapes=[
            VMEM((1, count), jnp.int32), VMEM((1, count), jnp.int32),
            VMEM((levels, count), F32), VMEM((1, count), F32),
            VMEM((levels, width, rows), F32),
            VMEM((levels, width, rows), BF), VMEM((levels, width, rows), BF),
            VMEM((1, CAPS), jnp.int32),
            VMEM((nlon, 2 * KMAX), F32), VMEM((2 * KMAX, nlon), F32),
            VMEM((lanes, FIELDS, slots), BF), VMEM((lanes, FIELDS, slots), BF),
            VMEM((lanes, 2, width, CAPS), BF), VMEM((lanes, 2, width, CAPS), BF),
            VMEM((lanes, width, CAPS), F32), VMEM((lanes, width, CAPS), F32),
            VMEM((lanes, width, CAPS), F32), VMEM((lanes, width, CAPS), F32),
            VMEM((lanes, width, CAPS), F32), VMEM((width, CAPS), F32),
            VMEM((3, levels, rows), BF), VMEM((2, levels, rows), BF),
            VMEM((3, levels, rows), BF), VMEM((2, levels, rows), BF),
            VMEM((2, levels, rows), F32), VMEM((2, levels, rows), F32),
            VMEM((2, levels, rows), F32), VMEM((2, levels, rows), F32),
            VMEM((levels * width, lanes * slots), BF), VMEM((1, lanes * slots), F32),
            VMEM((5, levels, rows), F32),
            VMEM((levels, width, rows), F32), VMEM((width, rows), F32),
            pltpu.SemaphoreType.DMA((10,)), pltpu.SemaphoreType.DMA((levels + 3,)),
            pltpu.SemaphoreType.DMA((4, lanes)), pltpu.SemaphoreType.DMA((4, lanes)),
            pltpu.SemaphoreType.DMA((lanes,)),
            pltpu.SemaphoreType.DMA((4,)), pltpu.SemaphoreType.DMA((4,)),
        ],
        compiler_params=pltpu.CompilerParams(
            vmem_limit_bytes=LIMIT, collective_id=0, has_side_effects=True
        ),
        name="window",
    )(
        sound_tile.reshape(1, count), sound_cell.reshape(1, count), sound_kernel,
        sound_weight.reshape(1, count), carry, east, north, cut, jnp.asarray(table),
        jnp.asarray(table.T.copy()),
    )


def extended(x, sides, width):
    for axis, dim in sides:
        devices, length = (lax.axis_size(axis), x.shape[dim])
        up = [(i, (i + 1) % devices) for i in range(devices)]
        down = [(j, i) for i, j in up]
        last = lax.slice_in_dim(x, length - width, length, axis=dim)
        initial = lax.slice_in_dim(x, 0, width, axis=dim)
        before = lax.ppermute(last, axis, up)
        after = lax.ppermute(initial, axis, down)
        x = jnp.concatenate([before, x, after], axis=dim)
    return x


def shifted(block, axis, distance):
    devices = range(lax.axis_size(axis))
    route = [((i - distance) % len(devices), i) for i in devices]
    return lax.ppermute(block, axis, route)


def wave_table(longitudes, nlon):
    waves = jnp.arange(KMAX, dtype=jnp.int32)
    phase = longitudes[:, None] * waves[None, :] % nlon
    angle = phase.astype(jnp.float32) * (2.0 * math.pi / nlon)
    return jnp.concatenate([jnp.cos(angle), jnp.sin(angle)], axis=1)


def wave_scale(cut_rows, nlon):
    waves = jnp.arange(KMAX, dtype=jnp.int32)
    factor = jnp.where(waves == 0, 1.0, 2.0) / nlon
    kept = jnp.where(waves[None, :] <= cut_rows[:, None], factor[None, :], 0.0).astype(jnp.float32)
    return jnp.concatenate([kept, kept], axis=1)


def spectral(polar, cutoff):
    levels, width, caps = polar.shape
    lanes = lax.axis_size("lon")
    me = lax.axis_index("lon")
    nlon = width * lanes
    table = wave_table(me * width + jnp.arange(width, dtype=jnp.int32), nlon)
    partial_coef = jnp.einsum("lwr,wk->lrk", polar, table, precision=HIGH)
    total = lax.psum(partial_coef, "lon")
    scale = wave_scale(cutoff, nlon)
    return jnp.einsum("lrk,wk->lwr", total * scale[None], table, precision=HIGH)


def transport(padded, east, west, north, south):
    field = padded[:, 1:-1]
    right = padded[:, 2:]
    left = padded[:, :-2]
    column = jnp.zeros_like(field[:, :, :1])
    upper = jnp.concatenate([field[:, :, 1:], column], axis=2)
    lower = jnp.concatenate([column, field[:, :, :-1]], axis=2)
    out = field + jnp.maximum(east, 0) * (right - field) + jnp.minimum(west, 0) * (field - left)
    return out + jnp.maximum(north, 0) * (upper - field) + jnp.minimum(south, 0) * (field - lower)


def adjoint_step(field, cutoff, east, west, north, south):
    rows = field.shape[2]
    polar = jnp.concatenate([field[:, :, :POLAR], field[:, :, rows - POLAR :]], axis=2)
    smooth = spectral(polar, cutoff)
    filtered = jnp.concatenate(
        [smooth[:, :, :POLAR], field[:, :, POLAR : rows - POLAR], smooth[:, :, POLAR:]], axis=2
    )
    padded = extended(filtered, (("lon", 1),), 1)
    return transport(padded, east, west, north, south)


def any_lanes(
    carry_adjoint,
    east_courant,
    north_courant,
    sound_tile,
    sound_cell,
    sound_kernel,
    sound_weight,
    cutoff,
):
    levels, width, rows = carry_adjoint.shape
    lanes = lax.axis_size("lon")
    count = sound_weight.shape[0]
    slots = max(2, 4 * count // lanes)
    target = sound_tile[:, 0]
    onehot = (target[:, None] == jnp.arange(lanes, dtype=jnp.int32)[None, :]).astype(jnp.int32)
    rank = jnp.sum((jnp.cumsum(onehot, axis=0) - 1) * onehot, axis=1)
    position = target * slots + rank
    values = sound_kernel * sound_weight[None, :]
    outgoing = jnp.zeros((levels, lanes * slots), jnp.float32).at[:, position].set(values)
    places = jnp.zeros((lanes * slots,), jnp.int32).at[position].set(sound_cell)
    arrived, spots = (
        lax.all_to_all(
            outgoing.reshape(levels, lanes, slots).astype(jnp.bfloat16),
            "lon",
            split_axis=1,
            concat_axis=1,
            tiled=True,
        ).astype(jnp.float32),
        lax.all_to_all(
            places.reshape(1, lanes, slots), "lon", split_axis=1, concat_axis=1, tiled=True
        ),
    )
    forcing = (
        jnp.zeros((levels, width * rows), jnp.float32)
        .at[:, spots.reshape(-1)]
        .add(arrived.reshape(levels, -1))
    )
    final_adjoint = carry_adjoint + forcing.reshape(levels, width, rows)
    west_face = shifted(east_courant[:, width - 1 :, :], "lon", 1)
    west_courant = jnp.concatenate([west_face, east_courant[:, :-1, :]], axis=1)
    row_index = jnp.arange(rows, dtype=jnp.int32)
    north = jnp.where(
        row_index[None, None, :] < rows - 1, north_courant, jnp.zeros_like(north_courant)
    )
    south = jnp.concatenate([jnp.zeros_like(north[:, :, :1]), north[:, :, :-1]], axis=2)
    mid_adjoint = adjoint_step(final_adjoint, cutoff, east_courant, west_courant, north, south)
    initial_adjoint = adjoint_step(mid_adjoint, cutoff, east_courant, west_courant, north, south)
    flux_grad = final_adjoint[0] + mid_adjoint[0]
    return (initial_adjoint, flux_grad)


def per_device(*arrays):
    if arrays[0].shape[0] == lax.axis_size("lon"):
        return levels_spread(*arrays)
    return any_lanes(*arrays)


def solution(mesh):
    in_specs = (
        P("parts", "lon", None),
        P("parts", "lon", None),
        P("parts", "lon", None),
        P(("parts", "lon"), None),
        P(("parts", "lon")),
        P("parts", "lon"),
        P(("parts", "lon")),
        P(),
    )
    out_specs = (P("parts", "lon", None), P(("parts", "lon"), None))
    return jax.shard_map(
        per_device, mesh=mesh, in_specs=in_specs, out_specs=out_specs, check_vma=False
    )
```

```python
import functools
import math

import jax
import jax.numpy as jnp
import numpy as np
from jax import lax
from jax.experimental import pallas as pl
from jax.experimental.pallas import tpu as pltpu
from jax.sharding import PartitionSpec as P

POLAR = 64
KMAX = 64
CAPS = 256
KEEP = 66
FIELDS = 32

HIGH = lax.Precision.HIGHEST
VMEM = pltpu.VMEM
BF = jnp.bfloat16
F32 = jnp.float32


def nt_dot(a, b):
    return lax.dot_general(a, b, (((1,), (1,)), ((), ())), preferred_element_type=F32)


def along_rows(field, north):
    rows = field.shape[-1]
    axis = field.ndim - 1
    step = pltpu.roll(field, rows - 1, axis) - field
    lower = pltpu.roll(jnp.minimum(north, 0.0) * step, 1, axis)
    return jnp.maximum(north, 0.0) * step + lower


def closed(north):
    rows = north.shape[-1]
    row = lax.broadcasted_iota(jnp.int32, north.shape, north.ndim - 1)
    return jnp.where(row < rows - 1, north.astype(F32), 0.0)


class Exchange:
    def __init__(self, lanes, send, receive, send_sem, receive_sem):
        self.lanes, self.send, self.receive = lanes, send, receive
        self.send_sem, self.receive_sem = send_sem, receive_sem
        self.me = lax.axis_index("lon")

    def copy(self, k, slot):
        target = lax.rem(self.me + k, self.lanes)
        return pltpu.make_async_remote_copy(
            src_ref=self.send.at[target],
            dst_ref=self.receive.at[slot],
            send_sem=self.send_sem.at[k],
            recv_sem=self.receive_sem.at[k],
            device_id={"lon": target},
            device_id_type=pl.DeviceIdType.MESH,
        )

    def start(self):
        def one(k, _):
            self.copy(k, self.me).start()
            return 0

        lax.fori_loop(1, self.lanes, one, 0)
        self.receive[self.me] = self.send[self.me]

    def arrive(self):
        def one(k, _):
            self.copy(k, lax.rem(self.me + self.lanes - k, self.lanes)).wait_recv()
            return 0

        lax.fori_loop(1, self.lanes, one, 0)

    def leave(self):
        def one(k, _):
            self.copy(k, self.me).wait_send()
            return 0

        lax.fori_loop(1, self.lanes, one, 0)


def lane_of(x):
    return lax.broadcasted_iota(jnp.int32, x.shape, x.ndim - 1)


def folded(ref):
    rows, half = ref.shape[2], CAPS // 2
    first = ref[:, :, :half].astype(F32)
    last = ref[:, :, rows - half :].astype(F32)
    polar = lane_of(first) < POLAR
    return jnp.where(polar, first, last), jnp.where(polar, last, first)


def unfolded(main, rest):
    polar = lane_of(main) < POLAR
    return jnp.concatenate([jnp.where(polar, main, rest), jnp.where(polar, rest, main)], axis=2)


def pack(ref, main, rest):
    width = main.shape[1]
    ref[:, :width] = main
    extra = rest[:, :8]
    for g in range(1, width // 8):
        moved = pltpu.roll(rest[:, 8 * g : 8 * g + 8], 8 * g, 2)
        extra = jnp.where(lane_of(extra) < POLAR - 4 + 8 * g, extra, moved)
    ref[:, width:] = extra


def unpack(ref, width):
    extra = ref[:, width:]
    parts = [extra]
    for g in range(1, width // 8):
        parts.append(pltpu.roll(extra, CAPS // 2 - 8 * g, 2))
    return unfolded(ref[:, :width], jnp.concatenate(parts, axis=1))


def window_kernel(tile_hbm, cell_hbm, kernel_hbm, weight_hbm, carry_hbm, east_hbm, north_hbm,
                  cut_hbm, table_hbm, wide_hbm, initial_hbm, flux_hbm,
                  tile_ref, cell_ref, kernel_ref, weight_ref, final_ref, east_ref, north_ref,
                  cut_ref, table_ref, wide_ref, message, arrived, caps, courant, ends, circles,
                  back, returned, flux_send, flux_caps, to_right, to_left, from_west, from_east,
                  right_edge, left_edge, west_edge, east_edge, spread_ref, row_ref, edge_ref,
                  initial_ref, flux_ref, load_sem, store_sem, all_send, all_receive, flux_sems,
                  side_send, side_receive):
    levels, width, rows = carry_hbm.shape
    lanes, _, slots = message.shape
    half = CAPS // 2
    block = 256
    me = lax.axis_index("lon")
    right, left = lax.rem(me + 1, lanes), lax.rem(me + lanes - 1, lanes)
    pairs = [(tile_hbm, tile_ref), (cell_hbm, cell_ref), (weight_hbm, weight_ref),
             (kernel_hbm, kernel_ref), (east_hbm, east_ref), (north_hbm, north_ref),
             (carry_hbm, final_ref), (cut_hbm, cut_ref), (table_hbm, table_ref),
             (wide_hbm, wide_ref)]
    loads = [pltpu.make_async_copy(a, b, load_sem.at[i]) for i, (a, b) in enumerate(pairs)]
    for load in loads:
        load.start()

    barrier = pltpu.get_barrier_semaphore()

    def greet(k, _):
        pl.semaphore_signal(
            barrier, inc=1, device_id={"lon": lax.rem(me + k, lanes)},
            device_id_type=pl.DeviceIdType.MESH,
        )
        return 0

    lax.fori_loop(1, lanes, greet, 0)

    def side(send, receive, sem, target):
        return pltpu.make_async_remote_copy(
            src_ref=send, dst_ref=receive, send_sem=side_send.at[sem],
            recv_sem=side_receive.at[sem], device_id={"lon": target},
            device_id_type=pl.DeviceIdType.MESH,
        )

    for load in loads[:4]:
        load.wait()
    route(tile_ref, cell_ref, kernel_ref, weight_ref, message, rows)
    pl.semaphore_wait(barrier, lanes - 1)
    soundings = Exchange(lanes, message, arrived, all_send.at[0], all_receive.at[0])
    soundings.start()

    for load in loads[4:6]:
        load.wait()
    east_main, east_rest = folded(east_ref)
    north_main, north_rest = folded(north_ref)
    caps[:, 0] = east_main.astype(BF)
    caps[:, 1] = north_main.astype(BF)
    rest = jnp.where(lane_of(east_rest) < POLAR + 4, east_rest, pltpu.roll(north_rest, 8, 2))
    caps[:, 2] = rest.astype(BF)
    winds = Exchange(lanes, caps, courant, all_send.at[1], all_receive.at[1])
    winds.start()
    to_right[0] = east_ref[:, width - 2, :]
    to_right[1] = east_ref[:, width - 1, :]
    to_right[2] = north_ref[:, width - 1, :]
    to_left[0] = east_ref[:, 0, :]
    to_left[1] = north_ref[:, 0, :]
    wind_sides = [side(to_right, from_west, 0, right), side(to_left, from_east, 1, left)]
    for copy in wind_sides:
        copy.start()

    soundings.arrive()
    for d in range(lanes):
        part = arrived[d]
        at = pl.ds(d * slots, slots)
        wide = part[levels : levels + 8].astype(F32)
        row_ref[:, at] = wide[1:2] * 128.0 + wide[2:3]
        here = lax.broadcasted_iota(jnp.int32, (width, slots), 0).astype(F32) == wide[0:1]
        values = part[:levels].astype(F32)
        for l in range(levels):
            spread_ref[l * width : (l + 1) * width, at] = jnp.where(
                here, values[l : l + 1], 0.0
            ).astype(BF)
    loads[6].wait()

    def scatter(base):
        at = pl.ds(base, block)
        row = row_ref[...] - jnp.asarray(base, F32)
        row = jnp.where((row >= 0) & (row < block), row, -1.0).astype(BF)
        index = lax.broadcasted_iota(jnp.int32, (block, lanes * slots), 0).astype(F32).astype(BF)
        onehot = jnp.where(index == row, jnp.ones((), BF), jnp.zeros((), BF))
        forcing = nt_dot(spread_ref[...], onehot)
        final_ref[:, :, at] = final_ref[:, :, at] + forcing.reshape(levels, width, block)

    scatter(0)
    scatter(rows - block)
    pack(ends, *folded(final_ref))
    polar = Exchange(lanes, ends, circles, all_send.at[2], all_receive.at[2])
    polar.start()

    def middle_block(i, _):
        scatter(pl.multiple_of(i * block, block))
        return 0

    lax.fori_loop(1, rows // block - 1, middle_block, 0)
    right_edge[0] = final_ref[:, width - 2, :]
    right_edge[1] = final_ref[:, width - 1, :]
    left_edge[0] = final_ref[:, 0, :]
    left_edge[1] = final_ref[:, 1, :]
    field_sides = [side(right_edge, west_edge, 2, right), side(left_edge, east_edge, 3, left)]
    for copy in field_sides:
        copy.start()

    for load in loads[7:]:
        load.wait()
    winds.arrive()
    polar.arrive()
    polar_steps(circles, courant, cut_ref, table_ref, wide_ref, back, flux_send)
    answer = Exchange(lanes, back, returned, all_send.at[3], all_receive.at[3])
    answer.start()

    def flux_copy(k):
        return pltpu.make_async_remote_copy(
            src_ref=flux_send.at[k], dst_ref=flux_caps, send_sem=flux_sems.at[k],
            recv_sem=flux_sems.at[0], device_id={"lon": k},
            device_id_type=pl.DeviceIdType.MESH,
        )

    @pl.when(me == 0)
    def _():
        def one(k, _):
            flux_copy(k).start()
            return 0

        lax.fori_loop(1, lanes, one, 0)
        flux_caps[...] = flux_send[0]

    for copy in wind_sides + field_sides:
        copy.wait_recv()
    side_edges(west_edge, east_edge, from_west, from_east, left_edge, right_edge, to_right, edge_ref)

    inner = pl.ds(half, rows - CAPS)

    def store(l):
        return pltpu.make_async_copy(
            initial_ref.at[l, :, inner], initial_hbm.at[l, :, inner], store_sem.at[l]
        )

    def level(l, _):
        middle = band(l, final_ref, east_ref, north_ref, edge_ref, initial_ref)
        store(l).start()

        @pl.when(l == 0)
        def _():
            flux_ref[...] = final_ref[0] + middle

        return 0

    lax.fori_loop(0, levels, level, 0)
    answer.arrive()

    @pl.when(me != 0)
    def _():
        flux_copy(1).wait_recv()

    answers = unpack(returned, width)
    lane = lax.broadcasted_iota(jnp.int32, (width, half), 1)
    lasts = []
    for i, at in enumerate((pl.ds(0, half), pl.ds(rows - half, half))):
        inside = (lane if i == 0 else half - 1 - lane) < KEEP
        side_at = pl.ds(i * half, half)
        for l in range(levels):
            initial_ref[l, :, at] = jnp.where(
                inside, answers[l, :, i * half : (i + 1) * half], initial_ref[l, :, at]
            )
        flux_ref[:, at] = jnp.where(inside, flux_caps[:, side_at], flux_ref[:, at])
        lasts.append(pltpu.make_async_copy(
            initial_ref.at[:, :, at], initial_hbm.at[:, :, at], store_sem.at[levels + i]
        ))
        lasts[-1].start()
    lasts.append(pltpu.make_async_copy(flux_ref, flux_hbm, store_sem.at[levels + 2]))
    lasts[-1].start()

    for copy in wind_sides + field_sides:
        copy.wait_send()
    for exchange in (soundings, winds, polar, answer):
        exchange.leave()

    @pl.when(me == 0)
    def _():
        def one(k, _):
            flux_copy(k).wait_send()
            return 0

        lax.fori_loop(1, lanes, one, 0)

    def stored(l, _):
        store(l).wait()
        return 0

    lax.fori_loop(0, levels, stored, 0)
    for copy in lasts:
        copy.wait()


def route(tile_ref, cell_ref, kernel_ref, weight_ref, message, rows):
    lanes, _, slots = message.shape
    levels, count = kernel_ref.shape
    tile = tile_ref[...]
    cell = cell_ref[...]
    member = lax.broadcasted_iota(jnp.int32, (lanes, count), 0) == tile
    onehot = jnp.where(member, 1.0, 0.0)
    before = lax.broadcasted_iota(jnp.int32, (count, count), 0) < lax.broadcasted_iota(
        jnp.int32, (count, count), 1
    )
    earlier = jnp.dot(
        onehot.astype(BF), jnp.where(before, 1.0, 0.0).astype(BF), preferred_element_type=F32
    )
    rank = jnp.sum(onehot * earlier, axis=0, keepdims=True).astype(jnp.int32)
    place = lax.broadcasted_iota(jnp.int32, (slots, count), 0) == rank
    place = jnp.where(place, 1.0, 0.0).astype(BF)
    values = kernel_ref[...] * weight_ref[...]
    lon = cell // rows
    row = cell - lon * rows
    high = row // 128
    low = row - high * 128
    index = lax.broadcasted_iota(jnp.int32, (FIELDS - levels, count), 0)
    extra = jnp.where(index == 0, lon, jnp.where(index == 1, high, jnp.where(index == 2, low, 0)))
    fields = jnp.concatenate([values, extra.astype(F32)], axis=0)
    spread = [jnp.where(tile == d, fields, 0.0).astype(BF) for d in range(lanes)]
    routed = nt_dot(jnp.concatenate(spread, axis=0), place)
    message[...] = routed.astype(BF).reshape(lanes, FIELDS, slots)


def polar_steps(field_ref, courant_ref, cut_ref, table_ref, wide_ref, back_ref, flux_send):
    sources, width, lanes = flux_send.shape
    nlon = sources * width
    field = unpack(field_ref, width).reshape(nlon, lanes)
    rest = courant_ref[:, 2].astype(F32)
    east = unfolded(courant_ref[:, 0].astype(F32), rest).reshape(nlon, lanes)
    rest = pltpu.roll(rest, CAPS // 2 - 8, 2)
    north = closed(unfolded(courant_ref[:, 1].astype(F32), rest).reshape(nlon, lanes))
    wave = lax.broadcasted_iota(jnp.int32, (2 * KMAX, lanes), 0)
    wave = jnp.where(wave >= KMAX, wave - KMAX, wave)
    factor = jnp.where(wave == 0, 1.0 / nlon, 2.0 / nlon)
    cut = cut_ref[...]
    scale = jnp.where(wave <= jnp.concatenate([cut, cut], axis=1), factor, 0.0)
    lane = lax.broadcasted_iota(jnp.int32, (nlon, lanes), 1)
    polar = (lane < POLAR) | (lane >= lanes - POLAR)

    def step(value):
        coef = jnp.dot(wide_ref[...], value, precision=HIGH, preferred_element_type=F32)
        smooth = jnp.dot(table_ref[...], coef * scale, precision=HIGH, preferred_element_type=F32)
        value = jnp.where(polar, smooth, value)
        change = pltpu.roll(value, nlon - 1, 0) - value
        west = pltpu.roll(jnp.minimum(east, 0.0) * change, 1, 0)
        return value + jnp.maximum(east, 0.0) * change + west + along_rows(value, north)

    middle = step(field)
    flux_send[...] = (field + middle).reshape(sources, width, lanes)
    back = step(middle).reshape(sources, width, lanes)
    pack(back_ref, *folded(back))


def up(x):
    return jnp.maximum(x, 0.0)


def down(x):
    return jnp.minimum(x, 0.0)


def side_edges(west_ref, right_ref, west_courant_ref, right_courant_ref, left_edge, right_edge,
               to_right, edge_ref):
    near, far = west_ref[1], west_ref[0]
    own_first, own_last = left_edge[0], right_edge[1]
    change = own_first - near
    e_near = west_courant_ref[1].astype(F32)
    from_near = down(e_near) * change
    before = near + up(e_near) * change + down(west_courant_ref[0].astype(F32)) * (near - far)
    edge_ref[0] = from_near
    edge_ref[1] = before + along_rows(near, closed(west_courant_ref[2]))
    after, beyond = right_ref[0], right_ref[1]
    e_after = right_courant_ref[0].astype(F32)
    next_mid = after + up(e_after) * (beyond - after)
    next_mid += down(to_right[1].astype(F32)) * (after - own_last)
    edge_ref[2] = next_mid + along_rows(after, closed(right_courant_ref[1]))
    edge_ref[3] = after
    edge_ref[4] = down(e_near)


def band(l, final_ref, east_ref, north_ref, edge_ref, initial_ref):
    levels, width, rows = final_ref.shape
    row = pl.ds(l, 1)
    field = final_ref[l]
    east = east_ref[l].astype(F32)
    north = closed(north_ref[l])
    at = lax.broadcasted_iota(jnp.int32, (width, rows), 0)

    def step(value, right, west):
        right = jnp.where(at == width - 1, right, pltpu.roll(value, width - 1, 0))
        change = right - value
        west = jnp.where(at == 0, west, pltpu.roll(down(east) * change, 1, 0))
        return value + up(east) * change + west + along_rows(value, north)

    middle = step(field, edge_ref[3, row], edge_ref[0, row])
    west = edge_ref[4, row] * (middle[0:1] - edge_ref[1, row])
    initial_ref[l] = step(middle, edge_ref[2, row], west)
    return middle


def full_table(nlon):
    phase = np.arange(nlon)[:, None] * np.arange(KMAX)[None, :] % nlon
    angle = phase * (2.0 * math.pi / nlon)
    return np.concatenate([np.cos(angle), np.sin(angle)], axis=1).astype(np.float32)


LIMIT = 56 * 1024 * 1024


def levels_spread(carry, east, north, sound_tile, sound_cell, sound_kernel, sound_weight, cutoff):
    levels, width, rows = carry.shape
    lanes = lax.axis_size("lon")
    nlon = lanes * width
    count = sound_weight.shape[0]
    slots = max(2, 4 * count // lanes)
    shape = jax.ShapeDtypeStruct
    table = full_table(nlon)
    cut = cutoff.reshape(1, 2 * POLAR)
    anywhere = pl.BlockSpec(memory_space=pl.ANY)
    return pl.pallas_call(
        window_kernel,
        out_shape=(shape((levels, width, rows), F32), shape((width, rows), F32)),
        in_specs=[anywhere] * 10,
        out_specs=(anywhere,) * 2,
        scratch_shapes=[
            VMEM((1, count), jnp.int32), VMEM((1, count), jnp.int32),
            VMEM((levels, count), F32), VMEM((1, count), F32),
            VMEM((levels, width, rows), F32),
            VMEM((levels, width, rows), BF), VMEM((levels, width, rows), BF),
            VMEM((1, 2 * POLAR), jnp.int32),
            VMEM((nlon, 2 * KMAX), F32), VMEM((2 * KMAX, nlon), F32),
            VMEM((lanes, FIELDS, slots), BF), VMEM((lanes, FIELDS, slots), BF),
            VMEM((lanes, 3, width, CAPS // 2), BF), VMEM((lanes, 3, width, CAPS // 2), BF),
            VMEM((lanes, width + 8, CAPS // 2), F32), VMEM((lanes, width + 8, CAPS // 2), F32),
            VMEM((lanes, width + 8, CAPS // 2), F32), VMEM((lanes, width + 8, CAPS // 2), F32),
            VMEM((lanes, width, CAPS), F32), VMEM((width, CAPS), F32),
            VMEM((3, levels, rows), BF), VMEM((2, levels, rows), BF),
            VMEM((3, levels, rows), BF), VMEM((2, levels, rows), BF),
            VMEM((2, levels, rows), F32), VMEM((2, levels, rows), F32),
            VMEM((2, levels, rows), F32), VMEM((2, levels, rows), F32),
            VMEM((levels * width, lanes * slots), BF), VMEM((1, lanes * slots), F32),
            VMEM((5, levels, rows), F32),
            VMEM((levels, width, rows), F32), VMEM((width, rows), F32),
            pltpu.SemaphoreType.DMA((10,)), pltpu.SemaphoreType.DMA((levels + 3,)),
            pltpu.SemaphoreType.DMA((4, lanes)), pltpu.SemaphoreType.DMA((4, lanes)),
            pltpu.SemaphoreType.DMA((lanes,)),
            pltpu.SemaphoreType.DMA((4,)), pltpu.SemaphoreType.DMA((4,)),
        ],
        compiler_params=pltpu.CompilerParams(
            vmem_limit_bytes=LIMIT, collective_id=0, has_side_effects=True
        ),
        name="window",
    )(
        sound_tile.reshape(1, count), sound_cell.reshape(1, count), sound_kernel,
        sound_weight.reshape(1, count), carry, east, north, cut, jnp.asarray(table),
        jnp.asarray(table.T.copy()),
    )


def extended(x, sides, width):
    for axis, dim in sides:
        devices, length = (lax.axis_size(axis), x.shape[dim])
        up = [(i, (i + 1) % devices) for i in range(devices)]
        down = [(j, i) for i, j in up]
        last = lax.slice_in_dim(x, length - width, length, axis=dim)
        initial = lax.slice_in_dim(x, 0, width, axis=dim)
        before = lax.ppermute(last, axis, up)
        after = lax.ppermute(initial, axis, down)
        x = jnp.concatenate([before, x, after], axis=dim)
    return x


def shifted(block, axis, distance):
    devices = range(lax.axis_size(axis))
    route = [((i - distance) % len(devices), i) for i in devices]
    return lax.ppermute(block, axis, route)


def wave_table(longitudes, nlon):
    waves = jnp.arange(KMAX, dtype=jnp.int32)
    phase = longitudes[:, None] * waves[None, :] % nlon
    angle = phase.astype(jnp.float32) * (2.0 * math.pi / nlon)
    return jnp.concatenate([jnp.cos(angle), jnp.sin(angle)], axis=1)


def wave_scale(cut_rows, nlon):
    waves = jnp.arange(KMAX, dtype=jnp.int32)
    factor = jnp.where(waves == 0, 1.0, 2.0) / nlon
    kept = jnp.where(waves[None, :] <= cut_rows[:, None], factor[None, :], 0.0).astype(jnp.float32)
    return jnp.concatenate([kept, kept], axis=1)


def spectral(polar, cutoff):
    levels, width, caps = polar.shape
    lanes = lax.axis_size("lon")
    me = lax.axis_index("lon")
    nlon = width * lanes
    table = wave_table(me * width + jnp.arange(width, dtype=jnp.int32), nlon)
    partial_coef = jnp.einsum("lwr,wk->lrk", polar, table, precision=HIGH)
    total = lax.psum(partial_coef, "lon")
    scale = wave_scale(cutoff, nlon)
    return jnp.einsum("lrk,wk->lwr", total * scale[None], table, precision=HIGH)


def transport(padded, east, west, north, south):
    field = padded[:, 1:-1]
    right = padded[:, 2:]
    left = padded[:, :-2]
    column = jnp.zeros_like(field[:, :, :1])
    upper = jnp.concatenate([field[:, :, 1:], column], axis=2)
    lower = jnp.concatenate([column, field[:, :, :-1]], axis=2)
    out = field + jnp.maximum(east, 0) * (right - field) + jnp.minimum(west, 0) * (field - left)
    return out + jnp.maximum(north, 0) * (upper - field) + jnp.minimum(south, 0) * (field - lower)


def adjoint_step(field, cutoff, east, west, north, south):
    rows = field.shape[2]
    polar = jnp.concatenate([field[:, :, :POLAR], field[:, :, rows - POLAR :]], axis=2)
    smooth = spectral(polar, cutoff)
    filtered = jnp.concatenate(
        [smooth[:, :, :POLAR], field[:, :, POLAR : rows - POLAR], smooth[:, :, POLAR:]], axis=2
    )
    padded = extended(filtered, (("lon", 1),), 1)
    return transport(padded, east, west, north, south)


def any_lanes(
    carry_adjoint,
    east_courant,
    north_courant,
    sound_tile,
    sound_cell,
    sound_kernel,
    sound_weight,
    cutoff,
):
    levels, width, rows = carry_adjoint.shape
    lanes = lax.axis_size("lon")
    count = sound_weight.shape[0]
    slots = max(2, 4 * count // lanes)
    target = sound_tile[:, 0]
    onehot = (target[:, None] == jnp.arange(lanes, dtype=jnp.int32)[None, :]).astype(jnp.int32)
    rank = jnp.sum((jnp.cumsum(onehot, axis=0) - 1) * onehot, axis=1)
    position = target * slots + rank
    values = sound_kernel * sound_weight[None, :]
    outgoing = jnp.zeros((levels, lanes * slots), jnp.float32).at[:, position].set(values)
    places = jnp.zeros((lanes * slots,), jnp.int32).at[position].set(sound_cell)
    arrived, spots = (
        lax.all_to_all(
            outgoing.reshape(levels, lanes, slots).astype(jnp.bfloat16),
            "lon",
            split_axis=1,
            concat_axis=1,
            tiled=True,
        ).astype(jnp.float32),
        lax.all_to_all(
            places.reshape(1, lanes, slots), "lon", split_axis=1, concat_axis=1, tiled=True
        ),
    )
    forcing = (
        jnp.zeros((levels, width * rows), jnp.float32)
        .at[:, spots.reshape(-1)]
        .add(arrived.reshape(levels, -1))
    )
    final_adjoint = carry_adjoint + forcing.reshape(levels, width, rows)
    west_face = shifted(east_courant[:, width - 1 :, :], "lon", 1)
    west_courant = jnp.concatenate([west_face, east_courant[:, :-1, :]], axis=1)
    row_index = jnp.arange(rows, dtype=jnp.int32)
    north = jnp.where(
        row_index[None, None, :] < rows - 1, north_courant, jnp.zeros_like(north_courant)
    )
    south = jnp.concatenate([jnp.zeros_like(north[:, :, :1]), north[:, :, :-1]], axis=2)
    mid_adjoint = adjoint_step(final_adjoint, cutoff, east_courant, west_courant, north, south)
    initial_adjoint = adjoint_step(mid_adjoint, cutoff, east_courant, west_courant, north, south)
    flux_grad = final_adjoint[0] + mid_adjoint[0]
    return (initial_adjoint, flux_grad)


def per_device(*arrays):
    if arrays[0].shape[0] == lax.axis_size("lon"):
        return levels_spread(*arrays)
    return any_lanes(*arrays)


def solution(mesh):
    in_specs = (
        P("parts", "lon", None),
        P("parts", "lon", None),
        P("parts", "lon", None),
        P(("parts", "lon"), None),
        P(("parts", "lon")),
        P("parts", "lon"),
        P(("parts", "lon")),
        P(),
    )
    out_specs = (P("parts", "lon", None), P(("parts", "lon"), None))
    return jax.shard_map(
        per_device, mesh=mesh, in_specs=in_specs, out_specs=out_specs, check_vma=False
    )
```

```python
import functools
import math

import jax
import jax.numpy as jnp
import numpy as np
from jax import lax
from jax.experimental import pallas as pl
from jax.experimental.pallas import tpu as pltpu
from jax.sharding import PartitionSpec as P

POLAR = 64
KMAX = 64
CAPS = 256
KEEP = 66
FIELDS = 24

HIGH = lax.Precision.HIGHEST
VMEM = pltpu.VMEM
BF = jnp.bfloat16
F32 = jnp.float32


def nt_dot(a, b):
    return lax.dot_general(a, b, (((1,), (1,)), ((), ())), preferred_element_type=F32)


def along_rows(field, north):
    rows = field.shape[-1]
    axis = field.ndim - 1
    step = pltpu.roll(field, rows - 1, axis) - field
    lower = pltpu.roll(jnp.minimum(north, 0.0) * step, 1, axis)
    return jnp.maximum(north, 0.0) * step + lower


def closed(north):
    rows = north.shape[-1]
    row = lax.broadcasted_iota(jnp.int32, north.shape, north.ndim - 1)
    return jnp.where(row < rows - 1, north.astype(F32), 0.0)


class Exchange:
    def __init__(self, lanes, send, receive, send_sem, receive_sem):
        self.lanes, self.send, self.receive = lanes, send, receive
        self.send_sem, self.receive_sem = send_sem, receive_sem
        self.me = lax.axis_index("lon")

    def copy(self, k, slot):
        target = lax.rem(self.me + k, self.lanes)
        return pltpu.make_async_remote_copy(
            src_ref=self.send.at[target],
            dst_ref=self.receive.at[slot],
            send_sem=self.send_sem.at[k],
            recv_sem=self.receive_sem.at[k],
            device_id={"lon": target},
            device_id_type=pl.DeviceIdType.MESH,
        )

    def start(self):
        def one(k, _):
            self.copy(k, self.me).start()
            return 0

        lax.fori_loop(1, self.lanes, one, 0)
        self.receive[self.me] = self.send[self.me]

    def arrive(self):
        def one(k, _):
            self.copy(k, lax.rem(self.me + self.lanes - k, self.lanes)).wait_recv()
            return 0

        lax.fori_loop(1, self.lanes, one, 0)

    def leave(self):
        def one(k, _):
            self.copy(k, self.me).wait_send()
            return 0

        lax.fori_loop(1, self.lanes, one, 0)


def lane_of(x):
    return lax.broadcasted_iota(jnp.int32, x.shape, x.ndim - 1)


def folded(ref):
    rows, half = ref.shape[2], CAPS // 2
    first = ref[:, :, :half].astype(F32)
    last = ref[:, :, rows - half :].astype(F32)
    polar = lane_of(first) < POLAR
    return jnp.where(polar, first, last), jnp.where(polar, last, first)


def unfolded(main, rest):
    polar = lane_of(main) < POLAR
    return jnp.concatenate([jnp.where(polar, main, rest), jnp.where(polar, rest, main)], axis=2)


def pack(ref, main, rest):
    width = main.shape[1]
    ref[:, :width] = main
    extra = rest[:, :8]
    for g in range(1, width // 8):
        moved = pltpu.roll(rest[:, 8 * g : 8 * g + 8], 8 * g, 2)
        extra = jnp.where(lane_of(extra) < POLAR - 4 + 8 * g, extra, moved)
    ref[:, width:] = extra


def unpack(ref, width):
    extra = ref[:, width:]
    parts = [extra]
    for g in range(1, width // 8):
        parts.append(pltpu.roll(extra, CAPS // 2 - 8 * g, 2))
    return unfolded(ref[:, :width], jnp.concatenate(parts, axis=1))


def window_kernel(tile_hbm, cell_hbm, kernel_hbm, weight_hbm, carry_hbm, east_hbm, north_hbm,
                  cut_hbm, table_hbm, wide_hbm, initial_hbm, flux_hbm,
                  tile_ref, cell_ref, kernel_ref, weight_ref, final_ref, east_ref, north_ref,
                  cut_ref, table_ref, wide_ref, message, arrived, caps, courant, ends, circles,
                  back, returned, flux_send, flux_caps, to_right, to_left, from_west, from_east,
                  right_edge, left_edge, west_edge, east_edge, spread_ref, row_ref, edge_ref,
                  initial_ref, flux_ref, load_sem, store_sem, all_send, all_receive, flux_sems,
                  side_send, side_receive):
    levels, width, rows = carry_hbm.shape
    lanes, _, slots = message.shape
    half = CAPS // 2
    block = 256
    me = lax.axis_index("lon")
    right, left = lax.rem(me + 1, lanes), lax.rem(me + lanes - 1, lanes)
    pairs = [(tile_hbm, tile_ref), (cell_hbm, cell_ref), (weight_hbm, weight_ref),
             (kernel_hbm, kernel_ref), (east_hbm, east_ref), (north_hbm, north_ref),
             (carry_hbm, final_ref), (cut_hbm, cut_ref), (table_hbm, table_ref),
             (wide_hbm, wide_ref)]
    loads = [pltpu.make_async_copy(a, b, load_sem.at[i]) for i, (a, b) in enumerate(pairs)]
    for load in loads:
        load.start()

    barrier = pltpu.get_barrier_semaphore()

    def greet(k, _):
        pl.semaphore_signal(
            barrier, inc=1, device_id={"lon": lax.rem(me + k, lanes)},
            device_id_type=pl.DeviceIdType.MESH,
        )
        return 0

    lax.fori_loop(1, lanes, greet, 0)

    def side(send, receive, sem, target):
        return pltpu.make_async_remote_copy(
            src_ref=send, dst_ref=receive, send_sem=side_send.at[sem],
            recv_sem=side_receive.at[sem], device_id={"lon": target},
            device_id_type=pl.DeviceIdType.MESH,
        )

    for load in loads[:4]:
        load.wait()
    route(tile_ref, cell_ref, kernel_ref, weight_ref, message, rows)
    pl.semaphore_wait(barrier, lanes - 1)
    soundings = Exchange(lanes, message, arrived, all_send.at[0], all_receive.at[0])
    soundings.start()

    for load in loads[4:6]:
        load.wait()
    east_main, east_rest = folded(east_ref)
    north_main, north_rest = folded(north_ref)
    caps[:, 0] = east_main.astype(BF)
    caps[:, 1] = north_main.astype(BF)
    rest = jnp.where(lane_of(east_rest) < POLAR + 4, east_rest, pltpu.roll(north_rest, 8, 2))
    caps[:, 2] = rest.astype(BF)
    winds = Exchange(lanes, caps, courant, all_send.at[1], all_receive.at[1])
    winds.start()
    to_right[0] = east_ref[:, width - 2, :]
    to_right[1] = east_ref[:, width - 1, :]
    to_right[2] = north_ref[:, width - 1, :]
    to_left[0] = east_ref[:, 0, :]
    to_left[1] = north_ref[:, 0, :]
    wind_sides = [side(to_right, from_west, 0, right), side(to_left, from_east, 1, left)]
    for copy in wind_sides:
        copy.start()

    soundings.arrive()
    for d in range(lanes):
        part = arrived[d]
        at = pl.ds(d * slots, slots)
        wide = part[levels : levels + 8].astype(F32)
        row_ref[:, at] = wide[1:2] * 128.0 + wide[2:3]
        here = lax.broadcasted_iota(jnp.int32, (width, slots), 0).astype(F32) == wide[0:1]
        values = part[:levels].astype(F32)
        for l in range(levels):
            spread_ref[l * width : (l + 1) * width, at] = jnp.where(
                here, values[l : l + 1], 0.0
            ).astype(BF)
    loads[6].wait()

    def scatter(base):
        at = pl.ds(base, block)
        row = row_ref[...] - jnp.asarray(base, F32)
        row = jnp.where((row >= 0) & (row < block), row, -1.0).astype(BF)
        index = lax.broadcasted_iota(jnp.int32, (block, lanes * slots), 0).astype(F32).astype(BF)
        onehot = jnp.where(index == row, jnp.ones((), BF), jnp.zeros((), BF))
        forcing = nt_dot(spread_ref[...], onehot)
        final_ref[:, :, at] = final_ref[:, :, at] + forcing.reshape(levels, width, block)

    scatter(0)
    scatter(rows - block)
    pack(ends, *folded(final_ref))
    polar = Exchange(lanes, ends, circles, all_send.at[2], all_receive.at[2])
    polar.start()

    def middle_block(i, _):
        scatter(pl.multiple_of(i * block, block))
        return 0

    lax.fori_loop(1, rows // block - 1, middle_block, 0)
    right_edge[0] = final_ref[:, width - 2, :]
    right_edge[1] = final_ref[:, width - 1, :]
    left_edge[0] = final_ref[:, 0, :]
    left_edge[1] = final_ref[:, 1, :]
    field_sides = [side(right_edge, west_edge, 2, right), side(left_edge, east_edge, 3, left)]
    for copy in field_sides:
        copy.start()

    for load in loads[7:]:
        load.wait()
    winds.arrive()
    polar.arrive()
    polar_steps(circles, courant, cut_ref, table_ref, wide_ref, back, flux_send)
    answer = Exchange(lanes, back, returned, all_send.at[3], all_receive.at[3])
    answer.start()

    def flux_copy(k):
        return pltpu.make_async_remote_copy(
            src_ref=flux_send.at[k], dst_ref=flux_caps, send_sem=flux_sems.at[k],
            recv_sem=flux_sems.at[0], device_id={"lon": k},
            device_id_type=pl.DeviceIdType.MESH,
        )

    @pl.when(me == 0)
    def _():
        def one(k, _):
            flux_copy(k).start()
            return 0

        lax.fori_loop(1, lanes, one, 0)
        flux_caps[...] = flux_send[0]

    for copy in wind_sides + field_sides:
        copy.wait_recv()
    side_edges(west_edge, east_edge, from_west, from_east, left_edge, right_edge, to_right, edge_ref)

    inner = pl.ds(half, rows - CAPS)

    def store(l):
        return pltpu.make_async_copy(
            initial_ref.at[l, :, inner], initial_hbm.at[l, :, inner], store_sem.at[l]
        )

    def level(l, _):
        middle = band(l, final_ref, east_ref, north_ref, edge_ref, initial_ref)
        store(l).start()

        @pl.when(l == 0)
        def _():
            flux_ref[...] = final_ref[0] + middle

        return 0

    lax.fori_loop(0, levels, level, 0)
    answer.arrive()

    @pl.when(me != 0)
    def _():
        flux_copy(1).wait_recv()

    answers = unpack(returned, width)
    lane = lax.broadcasted_iota(jnp.int32, (width, half), 1)
    lasts = []
    for i, at in enumerate((pl.ds(0, half), pl.ds(rows - half, half))):
        inside = (lane if i == 0 else half - 1 - lane) < KEEP
        side_at = pl.ds(i * half, half)
        for l in range(levels):
            initial_ref[l, :, at] = jnp.where(
                inside, answers[l, :, i * half : (i + 1) * half], initial_ref[l, :, at]
            )
        flux_ref[:, at] = jnp.where(inside, flux_caps[:, side_at], flux_ref[:, at])
        lasts.append(pltpu.make_async_copy(
            initial_ref.at[:, :, at], initial_hbm.at[:, :, at], store_sem.at[levels + i]
        ))
        lasts[-1].start()
    lasts.append(pltpu.make_async_copy(flux_ref, flux_hbm, store_sem.at[levels + 2]))
    lasts[-1].start()

    for copy in wind_sides + field_sides:
        copy.wait_send()
    for exchange in (soundings, winds, polar, answer):
        exchange.leave()

    @pl.when(me == 0)
    def _():
        def one(k, _):
            flux_copy(k).wait_send()
            return 0

        lax.fori_loop(1, lanes, one, 0)

    def stored(l, _):
        store(l).wait()
        return 0

    lax.fori_loop(0, levels, stored, 0)
    for copy in lasts:
        copy.wait()


def route(tile_ref, cell_ref, kernel_ref, weight_ref, message, rows):
    lanes, _, slots = message.shape
    levels, count = kernel_ref.shape
    tile = tile_ref[...]
    cell = cell_ref[...]
    member = lax.broadcasted_iota(jnp.int32, (lanes, count), 0) == tile
    onehot = jnp.where(member, 1.0, 0.0)
    before = lax.broadcasted_iota(jnp.int32, (count, count), 0) < lax.broadcasted_iota(
        jnp.int32, (count, count), 1
    )
    earlier = jnp.dot(
        onehot.astype(BF), jnp.where(before, 1.0, 0.0).astype(BF), preferred_element_type=F32
    )
    rank = jnp.sum(onehot * earlier, axis=0, keepdims=True).astype(jnp.int32)
    place = lax.broadcasted_iota(jnp.int32, (slots, count), 0) == rank
    place = jnp.where(place, 1.0, 0.0).astype(BF)
    values = kernel_ref[...] * weight_ref[...]
    lon = cell // rows
    row = cell - lon * rows
    high = row // 128
    low = row - high * 128
    index = lax.broadcasted_iota(jnp.int32, (FIELDS - levels, count), 0)
    extra = jnp.where(index == 0, lon, jnp.where(index == 1, high, jnp.where(index == 2, low, 0)))
    fields = jnp.concatenate([values, extra.astype(F32)], axis=0)
    spread = [jnp.where(tile == d, fields, 0.0).astype(BF) for d in range(lanes)]
    routed = nt_dot(jnp.concatenate(spread, axis=0), place)
    message[...] = routed.reshape(lanes, FIELDS, slots).astype(BF)


def polar_steps(field_ref, courant_ref, cut_ref, table_ref, wide_ref, back_ref, flux_send):
    sources, width, lanes = flux_send.shape
    nlon = sources * width
    field = unpack(field_ref, width).reshape(nlon, lanes)
    rest = courant_ref[:, 2].astype(F32)
    east = unfolded(courant_ref[:, 0].astype(F32), rest).reshape(nlon, lanes)
    rest = pltpu.roll(rest, CAPS // 2 - 8, 2)
    north = closed(unfolded(courant_ref[:, 1].astype(F32), rest).reshape(nlon, lanes))
    wave = lax.broadcasted_iota(jnp.int32, (2 * KMAX, lanes), 0)
    wave = jnp.where(wave >= KMAX, wave - KMAX, wave)
    factor = jnp.where(wave == 0, 1.0 / nlon, 2.0 / nlon)
    cut = cut_ref[...]
    scale = jnp.where(wave <= jnp.concatenate([cut, cut], axis=1), factor, 0.0)
    lane = lax.broadcasted_iota(jnp.int32, (nlon, lanes), 1)
    polar = (lane < POLAR) | (lane >= lanes - POLAR)

    def step(value):
        coef = jnp.dot(wide_ref[...], value, precision=HIGH, preferred_element_type=F32)
        smooth = jnp.dot(table_ref[...], coef * scale, precision=HIGH, preferred_element_type=F32)
        value = jnp.where(polar, smooth, value)
        change = pltpu.roll(value, nlon - 1, 0) - value
        west = pltpu.roll(jnp.minimum(east, 0.0) * change, 1, 0)
        return value + jnp.maximum(east, 0.0) * change + west + along_rows(value, north)

    middle = step(field)
    flux_send[...] = (field + middle).reshape(sources, width, lanes)
    back = step(middle).reshape(sources, width, lanes)
    pack(back_ref, *folded(back))


def up(x):
    return jnp.maximum(x, 0.0)


def down(x):
    return jnp.minimum(x, 0.0)


def side_edges(west_ref, right_ref, west_courant_ref, right_courant_ref, left_edge, right_edge,
               to_right, edge_ref):
    near, far = west_ref[1], west_ref[0]
    own_first, own_last = left_edge[0], right_edge[1]
    change = own_first - near
    e_near = west_courant_ref[1].astype(F32)
    from_near = down(e_near) * change
    before = near + up(e_near) * change + down(west_courant_ref[0].astype(F32)) * (near - far)
    edge_ref[0] = from_near
    edge_ref[1] = before + along_rows(near, closed(west_courant_ref[2]))
    after, beyond = right_ref[0], right_ref[1]
    e_after = right_courant_ref[0].astype(F32)
    next_mid = after + up(e_after) * (beyond - after)
    next_mid += down(to_right[1].astype(F32)) * (after - own_last)
    edge_ref[2] = next_mid + along_rows(after, closed(right_courant_ref[1]))
    edge_ref[3] = after
    edge_ref[4] = down(e_near)


def band(l, final_ref, east_ref, north_ref, edge_ref, initial_ref):
    levels, width, rows = final_ref.shape
    row = pl.ds(l, 1)
    field = final_ref[l]
    east = east_ref[l].astype(F32)
    north = closed(north_ref[l])
    at = lax.broadcasted_iota(jnp.int32, (width, rows), 0)

    def step(value, right, west):
        right = jnp.where(at == width - 1, right, pltpu.roll(value, width - 1, 0))
        change = right - value
        west = jnp.where(at == 0, west, pltpu.roll(down(east) * change, 1, 0))
        return value + up(east) * change + west + along_rows(value, north)

    middle = step(field, edge_ref[3, row], edge_ref[0, row])
    west = edge_ref[4, row] * (middle[0:1] - edge_ref[1, row])
    initial_ref[l] = step(middle, edge_ref[2, row], west)
    return middle


def full_table(nlon):
    phase = np.arange(nlon)[:, None] * np.arange(KMAX)[None, :] % nlon
    angle = phase * (2.0 * math.pi / nlon)
    return np.concatenate([np.cos(angle), np.sin(angle)], axis=1).astype(np.float32)


LIMIT = 56 * 1024 * 1024


def levels_spread(carry, east, north, sound_tile, sound_cell, sound_kernel, sound_weight, cutoff):
    levels, width, rows = carry.shape
    lanes = lax.axis_size("lon")
    nlon = lanes * width
    count = sound_weight.shape[0]
    slots = max(2, 4 * count // lanes)
    shape = jax.ShapeDtypeStruct
    table = full_table(nlon)
    cut = cutoff.reshape(1, 2 * POLAR)
    anywhere = pl.BlockSpec(memory_space=pl.ANY)
    return pl.pallas_call(
        window_kernel,
        out_shape=(shape((levels, width, rows), F32), shape((width, rows), F32)),
        in_specs=[anywhere] * 10,
        out_specs=(anywhere,) * 2,
        scratch_shapes=[
            VMEM((1, count), jnp.int32), VMEM((1, count), jnp.int32),
            VMEM((levels, count), F32), VMEM((1, count), F32),
            VMEM((levels, width, rows), F32),
            VMEM((levels, width, rows), BF), VMEM((levels, width, rows), BF),
            VMEM((1, 2 * POLAR), jnp.int32),
            VMEM((nlon, 2 * KMAX), F32), VMEM((2 * KMAX, nlon), F32),
            VMEM((lanes, FIELDS, slots), BF), VMEM((lanes, FIELDS, slots), BF),
            VMEM((lanes, 3, width, CAPS // 2), BF), VMEM((lanes, 3, width, CAPS // 2), BF),
            VMEM((lanes, width + 8, CAPS // 2), F32), VMEM((lanes, width + 8, CAPS // 2), F32),
            VMEM((lanes, width + 8, CAPS // 2), F32), VMEM((lanes, width + 8, CAPS // 2), F32),
            VMEM((lanes, width, CAPS), F32), VMEM((width, CAPS), F32),
            VMEM((3, levels, rows), BF), VMEM((2, levels, rows), BF),
            VMEM((3, levels, rows), BF), VMEM((2, levels, rows), BF),
            VMEM((2, levels, rows), F32), VMEM((2, levels, rows), F32),
            VMEM((2, levels, rows), F32), VMEM((2, levels, rows), F32),
            VMEM((levels * width, lanes * slots), BF), VMEM((1, lanes * slots), F32),
            VMEM((5, levels, rows), F32),
            VMEM((levels, width, rows), F32), VMEM((width, rows), F32),
            pltpu.SemaphoreType.DMA((10,)), pltpu.SemaphoreType.DMA((levels + 3,)),
            pltpu.SemaphoreType.DMA((4, lanes)), pltpu.SemaphoreType.DMA((4, lanes)),
            pltpu.SemaphoreType.DMA((lanes,)),
            pltpu.SemaphoreType.DMA((4,)), pltpu.SemaphoreType.DMA((4,)),
        ],
        compiler_params=pltpu.CompilerParams(
            vmem_limit_bytes=LIMIT, collective_id=0, has_side_effects=True
        ),
        name="window",
    )(
        sound_tile.reshape(1, count), sound_cell.reshape(1, count), sound_kernel,
        sound_weight.reshape(1, count), carry, east, north, cut, jnp.asarray(table),
        jnp.asarray(table.T.copy()),
    )


def extended(x, sides, width):
    for axis, dim in sides:
        devices, length = (lax.axis_size(axis), x.shape[dim])
        up = [(i, (i + 1) % devices) for i in range(devices)]
        down = [(j, i) for i, j in up]
        last = lax.slice_in_dim(x, length - width, length, axis=dim)
        initial = lax.slice_in_dim(x, 0, width, axis=dim)
        before = lax.ppermute(last, axis, up)
        after = lax.ppermute(initial, axis, down)
        x = jnp.concatenate([before, x, after], axis=dim)
    return x


def shifted(block, axis, distance):
    devices = range(lax.axis_size(axis))
    route = [((i - distance) % len(devices), i) for i in devices]
    return lax.ppermute(block, axis, route)


def wave_table(longitudes, nlon):
    waves = jnp.arange(KMAX, dtype=jnp.int32)
    phase = longitudes[:, None] * waves[None, :] % nlon
    angle = phase.astype(jnp.float32) * (2.0 * math.pi / nlon)
    return jnp.concatenate([jnp.cos(angle), jnp.sin(angle)], axis=1)


def wave_scale(cut_rows, nlon):
    waves = jnp.arange(KMAX, dtype=jnp.int32)
    factor = jnp.where(waves == 0, 1.0, 2.0) / nlon
    kept = jnp.where(waves[None, :] <= cut_rows[:, None], factor[None, :], 0.0).astype(jnp.float32)
    return jnp.concatenate([kept, kept], axis=1)


def spectral(polar, cutoff):
    levels, width, caps = polar.shape
    lanes = lax.axis_size("lon")
    me = lax.axis_index("lon")
    nlon = width * lanes
    table = wave_table(me * width + jnp.arange(width, dtype=jnp.int32), nlon)
    partial_coef = jnp.einsum("lwr,wk->lrk", polar, table, precision=HIGH)
    total = lax.psum(partial_coef, "lon")
    scale = wave_scale(cutoff, nlon)
    return jnp.einsum("lrk,wk->lwr", total * scale[None], table, precision=HIGH)


def transport(padded, east, west, north, south):
    field = padded[:, 1:-1]
    right = padded[:, 2:]
    left = padded[:, :-2]
    column = jnp.zeros_like(field[:, :, :1])
    upper = jnp.concatenate([field[:, :, 1:], column], axis=2)
    lower = jnp.concatenate([column, field[:, :, :-1]], axis=2)
    out = field + jnp.maximum(east, 0) * (right - field) + jnp.minimum(west, 0) * (field - left)
    return out + jnp.maximum(north, 0) * (upper - field) + jnp.minimum(south, 0) * (field - lower)


def adjoint_step(field, cutoff, east, west, north, south):
    rows = field.shape[2]
    polar = jnp.concatenate([field[:, :, :POLAR], field[:, :, rows - POLAR :]], axis=2)
    smooth = spectral(polar, cutoff)
    filtered = jnp.concatenate(
        [smooth[:, :, :POLAR], field[:, :, POLAR : rows - POLAR], smooth[:, :, POLAR:]], axis=2
    )
    padded = extended(filtered, (("lon", 1),), 1)
    return transport(padded, east, west, north, south)


def any_lanes(
    carry_adjoint,
    east_courant,
    north_courant,
    sound_tile,
    sound_cell,
    sound_kernel,
    sound_weight,
    cutoff,
):
    levels, width, rows = carry_adjoint.shape
    lanes = lax.axis_size("lon")
    count = sound_weight.shape[0]
    slots = max(2, 4 * count // lanes)
    target = sound_tile[:, 0]
    onehot = (target[:, None] == jnp.arange(lanes, dtype=jnp.int32)[None, :]).astype(jnp.int32)
    rank = jnp.sum((jnp.cumsum(onehot, axis=0) - 1) * onehot, axis=1)
    position = target * slots + rank
    values = sound_kernel * sound_weight[None, :]
    outgoing = jnp.zeros((levels, lanes * slots), jnp.float32).at[:, position].set(values)
    places = jnp.zeros((lanes * slots,), jnp.int32).at[position].set(sound_cell)
    arrived, spots = (
        lax.all_to_all(
            outgoing.reshape(levels, lanes, slots).astype(jnp.bfloat16),
            "lon",
            split_axis=1,
            concat_axis=1,
            tiled=True,
        ).astype(jnp.float32),
        lax.all_to_all(
            places.reshape(1, lanes, slots), "lon", split_axis=1, concat_axis=1, tiled=True
        ),
    )
    forcing = (
        jnp.zeros((levels, width * rows), jnp.float32)
        .at[:, spots.reshape(-1)]
        .add(arrived.reshape(levels, -1))
    )
    final_adjoint = carry_adjoint + forcing.reshape(levels, width, rows)
    west_face = shifted(east_courant[:, width - 1 :, :], "lon", 1)
    west_courant = jnp.concatenate([west_face, east_courant[:, :-1, :]], axis=1)
    row_index = jnp.arange(rows, dtype=jnp.int32)
    north = jnp.where(
        row_index[None, None, :] < rows - 1, north_courant, jnp.zeros_like(north_courant)
    )
    south = jnp.concatenate([jnp.zeros_like(north[:, :, :1]), north[:, :, :-1]], axis=2)
    mid_adjoint = adjoint_step(final_adjoint, cutoff, east_courant, west_courant, north, south)
    initial_adjoint = adjoint_step(mid_adjoint, cutoff, east_courant, west_courant, north, south)
    flux_grad = final_adjoint[0] + mid_adjoint[0]
    return (initial_adjoint, flux_grad)


def per_device(*arrays):
    if arrays[0].shape[0] == lax.axis_size("lon"):
        return levels_spread(*arrays)
    return any_lanes(*arrays)


def solution(mesh):
    in_specs = (
        P("parts", "lon", None),
        P("parts", "lon", None),
        P("parts", "lon", None),
        P(("parts", "lon"), None),
        P(("parts", "lon")),
        P("parts", "lon"),
        P(("parts", "lon")),
        P(),
    )
    out_specs = (P("parts", "lon", None), P(("parts", "lon"), None))
    return jax.shard_map(
        per_device, mesh=mesh, in_specs=in_specs, out_specs=out_specs, check_vma=False
    )
```
